512 devices in a mesh: rep: 8 (over z_hi, core), fsdp: 64 (over y, z_lo, x).
Axes of the slice: x: 4, y: 4, z: 16 (z_hi: 4, z_lo: 4; z = z_hi * 4 + z_lo), core: 2. Of those that a mesh axis runs over, the one named last changes fastest.
Arguments:
- gradients: bfloat16 [8, 64, 128, 5120], P('rep', 'fsdp'), may hold values from -2 to 2
- momentum: float32 [8, 128, 5120], P('rep', 'fsdp'), may hold values from -6 to 6
Outputs:
- new_momentum: float32 [8, 128, 5120], P('rep', 'fsdp')
- update: float32 [128, 5120], P('fsdp')
The draws below stay inside these ranges and needn't reach their ends.
All inputs are finite; a program needn't handle non-finite values.
Results may differ from the reference program's by a relative error of at most 0.0003.
Values sent between devices are 32-bit elements; how exact they have to be, the bound alone decides.
A program may use at most 64 MiB of HBM per device.

```python
import jax
import jax.numpy as jnp
from jax import lax

D = 5120
SPAN = 64
BAND = 8
ROWS = 128
SOURCES = 64
REPS = 8


def strengthened(values, key, source, target, parts, factor):
    owner, partner = [(jnp.arange(values.shape[axis_at]) // (values.shape[axis_at] // parts)).reshape([-1 if axis == axis_at else 1 for axis in range(values.ndim)]) for axis_at in (source, target)]
    chosen = jax.random.permutation(key, parts)[partner]
    strong = (owner == chosen) | (owner == (partner + parts // 2) % parts)
    return jnp.where(strong, factor * values, values)


def block_levels(own_key, shape, cuts, low, high):
    gain, own = 1.0, jax.random.fold_in(own_key, 6)
    for dim, parts in cuts:
        draws = jnp.exp(jax.random.uniform(jax.random.fold_in(own, dim), (parts,), jnp.float32, low / len(cuts), high / len(cuts)))
        gain = gain * jnp.repeat(draws, shape[dim] // parts).reshape([-1 if axis == dim else 1 for axis in range(len(shape))])
    return gain


def centred(rng, shape, spread, most, cuts=(), kind=jnp.bfloat16):
    result = jax.random.normal(rng, shape, jnp.float32) * spread
    if len(cuts) > 0:
        result = block_levels(rng, shape, cuts, -0.22, 0.18) * result
    return jnp.clip(result, min=-most, max=most).astype(kind)


def noise_with(rng, extent, spread, bound, cuts, heavy, kind=jnp.bfloat16):
    array = spread * jax.random.normal(rng, extent, jnp.float32)
    if cuts:
        array = array * block_levels(rng, extent, cuts, -0.22, 0.18)
    return jnp.clip(strengthened(array, jax.random.fold_in(rng, 3), *heavy), -bound, bound).astype(kind)


def setup_inputs(seed: int = 0) -> dict:
    streams_of = jax.random.split(jax.random.key(seed), 3)
    return {
        "gradients": noise_with(streams_of[0], (REPS, SOURCES, ROWS, D), 0.125, 2.0, ((0, 8), (1, 64)), (1, 2, 64, 4.0)),
        "momentum": centred(streams_of[1], (REPS, ROWS, D), 1.0, 6.0, ((0, 8), (1, 64)), jnp.float32),
    }


decay_rate = 0.9

def cosine_basis():
    freq = jnp.arange(BAND, dtype=jnp.float32)[:, None]
    place = jnp.arange(SPAN, dtype=jnp.float32)[None, :]
    table = jnp.cos(jnp.pi * (2.0 * place + 1.0) * freq / (2.0 * SPAN)) * jnp.sqrt(2.0 / SPAN)
    return table * jnp.where(freq == 0, jnp.sqrt(0.5), 1.0)

def reference(gradients, momentum):
    table = cosine_basis()

    def one_group(pair):
        group_grads, group_moment = pair
        summed = lax.optimization_barrier(jnp.sum(group_grads.astype(jnp.float32), axis=0))
        blended = decay_rate * group_moment + summed
        pieces = blended.reshape(ROWS, D // SPAN, SPAN)
        low_band = jnp.einsum('ikj,fj->ikf', pieces, table, precision=lax.Precision.HIGHEST)
        smooth = jnp.einsum('ikf,fj->ikj', low_band, table, precision=lax.Precision.HIGHEST)
        return ((pieces - smooth).reshape(ROWS, D), low_band)
    new_momentum, bands = lax.map(one_group, (gradients, momentum))
    band_total = lax.optimization_barrier(jnp.sum(bands, axis=0))
    update = jnp.einsum('ikf,fj->ikj', band_total, table, precision=lax.Precision.HIGHEST) / REPS
    return (new_momentum, update.reshape(ROWS, D))
```

```python
import jax
import jax.numpy as jnp
import ml_dtypes
import numpy as np
from jax import lax
from jax.experimental import pallas as pl
from jax.experimental.pallas import tpu as pltpu
from jax.sharding import PartitionSpec as P

SPAN = 64
BAND = 8
D = 5120
ROWS = 128
GROUP = 1024
GROUPS = D // GROUP
DECAY = 0.9
MESH = pl.DeviceIdType.MESH

CHUNKS = (
    ("zxy", 0, 1024),
    ("xyz", 1024, 1024),
    ("yxz", 2048, 1024),
    ("xyz", 3072, 1024),
    ("yxz", 4096, 1024),
)
N_CHUNKS = len(CHUNKS)
REPS = 8


def halves():
    freq = np.arange(BAND)[:, None]
    place = np.arange(SPAN)[None, :]
    table = np.cos(np.pi * (2.0 * place + 1.0) * freq / (2.0 * SPAN)) * np.sqrt(2.0 / SPAN)
    table = table * np.where(freq == 0, np.sqrt(0.5), 1.0)
    full = np.zeros((GROUP, GROUP // SPAN * BAND), np.float32)
    for block in range(GROUP // SPAN):
        full[block * SPAN : (block + 1) * SPAN, block * BAND : (block + 1) * BAND] = table.T
    high = full.astype(ml_dtypes.bfloat16)
    low = (full - high.astype(np.float32)).astype(ml_dtypes.bfloat16)
    return np.concatenate([high, low], axis=1)


def permutation(order):
    weight = {"y": 32, "z": 8, "x": 2}
    row = lax.broadcasted_iota(jnp.int32, (ROWS, ROWS), 0)
    column = lax.broadcasted_iota(jnp.int32, (ROWS, ROWS), 1)
    source = (
        ((row >> 5) & 3) * weight[order[0]]
        + ((row >> 3) & 3) * weight[order[1]]
        + ((row >> 1) & 3) * weight[order[2]]
        + (row & 1)
    )
    return jnp.where(source == column, 1.0, 0.0).astype(jnp.bfloat16)


def split(value):
    high = value.astype(jnp.bfloat16)
    return high, (value - high.astype(jnp.float32)).astype(jnp.bfloat16)


def analyse(value, basis_high, basis_low):
    high, low = split(value)
    dims = (((1,), (0,)), ((), ()))
    f32 = jnp.float32
    return (
        lax.dot_general(high, basis_high, dims, preferred_element_type=f32)
        + lax.dot_general(high, basis_low, dims, preferred_element_type=f32)
        + lax.dot_general(low, basis_high, dims, preferred_element_type=f32)
    )


def expand(value, basis_high, basis_low):
    high, low = split(value)
    dims = (((1,), (1,)), ((), ()))
    f32 = jnp.float32
    return (
        lax.dot_general(high, basis_high, dims, preferred_element_type=f32)
        + lax.dot_general(high, basis_low, dims, preferred_element_type=f32)
        + lax.dot_general(low, basis_high, dims, preferred_element_type=f32)
    )


def kernel(g_hbm, m_hbm, b_hbm, fresh_ref, update_ref, *scratch):
    scratch = list(scratch)
    g_ref, m_ref, b_ref, stack, bands = scratch[:5]
    per = scratch[5 : 5 + 6 * N_CHUNKS]
    load_sems, send_sems, recv_sems, rep_send, rep_recv = scratch[5 + 6 * N_CHUNKS :]

    rep = lax.axis_index("rep")
    fsdp = lax.axis_index("fsdp")
    at = {"y": fsdp // 16, "z": (fsdp // 4) % 4, "x": fsdp % 4}
    stride = {"y": 16, "z": 4, "x": 1}

    def peer(axis, k):
        there = lax.rem(at[axis] + k, 4)
        return there, {"rep": rep, "fsdp": fsdp + (there - at[axis]) * stride[axis]}

    def rep_peer(k):
        return {"rep": lax.rem(rep + k, REPS), "fsdp": fsdp}

    barrier = pltpu.get_barrier_semaphore()
    for k in range(1, REPS):
        pl.semaphore_signal(barrier, inc=1, device_id=rep_peer(k), device_id_type=MESH)
    for axis in "xyz":
        for k in range(1, 4):
            pl.semaphore_signal(barrier, inc=1, device_id=peer(axis, k)[1], device_id_type=MESH)

    loads = []
    for c, (order, first, width) in enumerate(CHUNKS):
        columns = pl.ds(first, width)
        loads.append(
            pltpu.make_async_copy(g_hbm.at[0, 0, :, columns], g_ref.at[:, columns], load_sems.at[c])
        )
        loads[-1].start()
    m_load = pltpu.make_async_copy(m_hbm.at[0], m_ref, load_sems.at[N_CHUNKS])
    b_load = pltpu.make_async_copy(b_hbm, b_ref, load_sems.at[N_CHUNKS + 1])
    m_load.start()
    b_load.start()

    turned = {order: permutation(order) for order in sorted({c[0] for c in CHUNKS})}
    stack[...] = jnp.zeros_like(stack)

    def copies(c, phase):
        order = CHUNKS[c][0]
        t_ref, s_ref, u_ref, r1, r2, r3 = per[6 * c : 6 * c + 6]
        result = []
        for k in range(1, 4):
            there, device = peer(order[phase], k)
            if phase == 0:
                source, target = t_ref.at[pl.ds(pl.multiple_of(there * 32, 32), 32)], r1.at[k - 1]
            elif phase == 1:
                source, target = s_ref.at[pl.ds(pl.multiple_of(there * 8, 8), 8)], r2.at[k - 1]
            else:
                source, target = u_ref.at[there], r3.at[k - 1]
            index = (c * 3 + phase) * 3 + k - 1
            result.append(
                pltpu.make_async_remote_copy(
                    src_ref=source,
                    dst_ref=target,
                    send_sem=send_sems.at[index],
                    recv_sem=recv_sems.at[index],
                    device_id=device,
                    device_id_type=MESH,
                )
            )
        return result

    def turn(c):
        order, first, width = CHUNKS[c]
        loads[c].wait()
        per[6 * c][...] = jnp.dot(
            turned[order], g_ref[:, first : first + width], preferred_element_type=jnp.float32
        )

    def go(c, phase):
        for copy in copies(c, phase):
            copy.start()

    turn(0)
    pl.semaphore_wait(barrier, REPS - 1 + 9)
    go(0, 0)
    for c in range(1, N_CHUNKS):
        turn(c)
        go(c, 0)

    def second(c):
        order, first, width = CHUNKS[c]
        t_ref, s_ref, u_ref, r1, r2, r3 = per[6 * c : 6 * c + 6]
        for copy in copies(c, 0):
            copy.wait_recv()
        own = pl.ds(pl.multiple_of(at[order[0]] * 32, 32), 32)
        s_ref[...] = (t_ref[own, :] + r1[0]) + (r1[1] + r1[2])
        go(c, 1)

    def third(c):
        order, first, width = CHUNKS[c]
        t_ref, s_ref, u_ref, r1, r2, r3 = per[6 * c : 6 * c + 6]
        for copy in copies(c, 1):
            copy.wait_recv()
        own = pl.ds(pl.multiple_of(at[order[1]] * 8, 8), 8)
        total = (s_ref[own, :] + r2[0]) + (r2[1] + r2[2])
        for q in range(4):
            u_ref[q] = total[2 * q : 2 * q + 2]
        go(c, 2)

    def last(c):
        order, first, width = CHUNKS[c]
        t_ref, s_ref, u_ref, r1, r2, r3 = per[6 * c : 6 * c + 6]
        for copy in copies(c, 2):
            copy.wait_recv()
        total = (u_ref[at[order[2]]] + r3[0]) + (r3[1] + r3[2])
        columns = slice(first, first + width)
        blended = DECAY * m_ref[:, columns] + total
        for part in range(width // GROUP):
            g = first // GROUP + part
            stack[2 * g : 2 * g + 2, :] = blended[:, part * GROUP : (part + 1) * GROUP]

    m_load.wait()
    b_load.wait()
    for step in range(N_CHUNKS + 2):
        if step < N_CHUNKS:
            second(step)
        if 0 <= step - 1 < N_CHUNKS:
            third(step - 1)
        if 0 <= step - 2 < N_CHUNKS:
            last(step - 2)

    high, low = b_ref[:, :128], b_ref[:, 128:]
    blended = stack[...]
    band = analyse(blended, high, low)
    bands[0] = band
    shares = []
    for k in range(1, REPS):
        copy = pltpu.make_async_remote_copy(
            src_ref=bands.at[0],
            dst_ref=bands.at[k],
            send_sem=rep_send.at[k - 1],
            recv_sem=rep_recv.at[k - 1],
            device_id=rep_peer(k),
            device_id_type=MESH,
        )
        copy.start()
        shares.append(copy)
    fresh = blended - expand(band, high, low)
    for g in range(GROUPS):
        fresh_ref[0, :, g * GROUP : (g + 1) * GROUP] = fresh[2 * g : 2 * g + 2]
    for copy in shares:
        copy.wait_recv()
    total = band
    for k in range(1, REPS):
        total = total + bands[k]
    update = expand(total * (1.0 / REPS), high, low)
    for g in range(GROUPS):
        update_ref[:, g * GROUP : (g + 1) * GROUP] = update[2 * g : 2 * g + 2]
    for c in range(N_CHUNKS):
        for phase in range(3):
            for copy in copies(c, phase):
                copy.wait_send()
    for copy in shares:
        copy.wait_send()


def shards(gradients, momentum):
    basis = jnp.asarray(halves())
    f32 = jnp.float32
    per = []
    for order, first, width in CHUNKS:
        per += [
            pltpu.VMEM((ROWS, width), f32),
            pltpu.VMEM((32, width), f32),
            pltpu.VMEM((4, 2, width), f32),
            pltpu.VMEM((3, 32, width), f32),
            pltpu.VMEM((3, 8, width), f32),
            pltpu.VMEM((3, 2, width), f32),
        ]
    return pl.pallas_call(
        kernel,
        out_shape=(
            jax.ShapeDtypeStruct((1, 2, D), f32),
            jax.ShapeDtypeStruct((2, D), f32),
        ),
        in_specs=[pl.BlockSpec(memory_space=pl.ANY)] * 3,
        out_specs=(pl.BlockSpec(memory_space=pltpu.VMEM),) * 2,
        scratch_shapes=[
            pltpu.VMEM((ROWS, D), jnp.bfloat16),
            pltpu.VMEM((2, D), f32),
            pltpu.VMEM((GROUP, 256), jnp.bfloat16),
            pltpu.VMEM((16, GROUP), f32),
            pltpu.VMEM((REPS, 16, 128), f32),
            *per,
            pltpu.SemaphoreType.DMA((N_CHUNKS + 2,)),
            pltpu.SemaphoreType.DMA((9 * N_CHUNKS,)),
            pltpu.SemaphoreType.DMA((9 * N_CHUNKS,)),
            pltpu.SemaphoreType.DMA((REPS - 1,)),
            pltpu.SemaphoreType.DMA((REPS - 1,)),
        ],
        compiler_params=pltpu.CompilerParams(
            collective_id=0, has_side_effects=True, vmem_limit_bytes=48 << 20
        ),
        name="momentum_step",
    )(gradients, momentum, basis)


def solution(mesh):
    return jax.shard_map(
        shards,
        mesh=mesh,
        in_specs=(P("rep", "fsdp", None, None), P("rep", "fsdp", None)),
        out_specs=(P("rep", "fsdp", None), P("fsdp", None)),
        check_vma=False,
    )
```

```python
import jax
import jax.numpy as jnp
import ml_dtypes
import numpy as np
from jax import lax
from jax.experimental import pallas as pl
from jax.experimental.pallas import tpu as pltpu
from jax.sharding import PartitionSpec as P

SPAN = 64
BAND = 8
D = 5120
ROWS = 128
GROUP = 1024
GROUPS = D // GROUP
DECAY = 0.9
MESH = pl.DeviceIdType.MESH

REPS = 8
RING = 16

CHUNKS = (
    ("xyz", 0, 512),
    ("yxz", 512, 512),
    ("zxy", 1024, 512),
    ("xyz", 1536, 896),
    ("yxz", 2432, 896),
    ("xyz", 3328, 896),
    ("yxz", 4224, 896),
)
N_CHUNKS = len(CHUNKS)
SETS = (("xyz", 0, 2), ("yxz", 2, 3))
BANDS = D // SPAN * BAND


def halves():
    freq = np.arange(BAND)[:, None]
    place = np.arange(SPAN)[None, :]
    table = np.cos(np.pi * (2.0 * place + 1.0) * freq / (2.0 * SPAN)) * np.sqrt(2.0 / SPAN)
    table = table * np.where(freq == 0, np.sqrt(0.5), 1.0)
    full = np.zeros((GROUP, GROUP // SPAN * BAND), np.float32)
    for block in range(GROUP // SPAN):
        full[block * SPAN : (block + 1) * SPAN, block * BAND : (block + 1) * BAND] = table.T
    high = full.astype(ml_dtypes.bfloat16)
    low = (full - high.astype(np.float32)).astype(ml_dtypes.bfloat16)
    return np.concatenate([high, low], axis=1)


def permutation(order):
    weight = {"y": 32, "z": 8, "x": 2}
    row = lax.broadcasted_iota(jnp.int32, (ROWS, ROWS), 0)
    column = lax.broadcasted_iota(jnp.int32, (ROWS, ROWS), 1)
    source = (
        ((row >> 5) & 3) * weight[order[0]]
        + ((row >> 3) & 3) * weight[order[1]]
        + ((row >> 1) & 3) * weight[order[2]]
        + (row & 1)
    )
    return jnp.where(source == column, 1.0, 0.0).astype(jnp.bfloat16)


def split(value):
    high = value.astype(jnp.bfloat16)
    return high, (value - high.astype(jnp.float32)).astype(jnp.bfloat16)


def analyse(value, basis_high, basis_low):
    high, low = split(value)
    dims = (((1,), (0,)), ((), ()))
    f32 = jnp.float32
    return (
        lax.dot_general(high, basis_high, dims, preferred_element_type=f32)
        + lax.dot_general(high, basis_low, dims, preferred_element_type=f32)
        + lax.dot_general(low, basis_high, dims, preferred_element_type=f32)
    )


def expand(value, basis_high, basis_low):
    high, low = split(value)
    dims = (((1,), (1,)), ((), ()))
    f32 = jnp.float32
    return (
        lax.dot_general(high, basis_high, dims, preferred_element_type=f32)
        + lax.dot_general(high, basis_low, dims, preferred_element_type=f32)
        + lax.dot_general(low, basis_high, dims, preferred_element_type=f32)
    )


def kernel(g_hbm, m_hbm, b_hbm, fresh_ref, update_ref, *scratch):
    scratch = list(scratch)
    take = lambda n: [scratch.pop(0) for _ in range(n)]
    g_ref, m_ref, b_ref, stack, band_stack = take(5)
    per = take(6 * N_CHUNKS)
    low_per = take(4 * len(SETS))
    ring_out, ring_in, pair_out, pair_in, old_ref = take(5)
    load_sems, send_sems, recv_sems, low_send, low_recv = take(5)
    ring_send, ring_recv, pair_send, pair_recv, relay = take(5)

    rep = lax.axis_index("rep")
    fsdp = lax.axis_index("fsdp")
    core = rep % 2
    at = {"y": fsdp // 16, "z": (fsdp // 4) % 4, "x": fsdp % 4}
    stride = {"y": 16, "z": 4, "x": 1}
    height = (rep // 2) * 4 + at["z"]

    def peer(axis, k):
        there = lax.rem(at[axis] + k, 4)
        return there, {"rep": rep, "fsdp": fsdp + (there - at[axis]) * stride[axis]}

    def ring_peer(k):
        there = lax.rem(height + k, RING)
        low = there % 4
        return low, {"rep": (there // 4) * 2 + core, "fsdp": fsdp + (low - at["z"]) * 4}

    other = {"rep": rep + 1 - 2 * core, "fsdp": fsdp}

    barrier = pltpu.get_barrier_semaphore()
    greeted = [ring_peer(k)[1] for k in (3, 13, 2, 14, 1, 15)]
    greeted += [peer(axis, k)[1] for k in (2, 1, 3) for axis in "xy"]
    greeted.append(other)
    for device in greeted:
        pl.semaphore_signal(barrier, inc=1, device_id=device, device_id_type=MESH)

    loads = []
    for g in range(GROUPS):
        columns = pl.ds(g * GROUP, GROUP)
        loads.append(
            pltpu.make_async_copy(g_hbm.at[0, 0, :, columns], g_ref.at[:, columns], load_sems.at[g])
        )
    b_load = pltpu.make_async_copy(b_hbm, b_ref, load_sems.at[GROUPS + 1])
    m_load = pltpu.make_async_copy(m_hbm.at[0], m_ref, load_sems.at[GROUPS])
    b_load.start()
    for load in loads:
        load.start()
    m_load.start()

    turned = {order: permutation(order) for order in ("xyz", "yxz", "zxy")}
    stack[...] = jnp.zeros_like(stack)
    band_stack[...] = jnp.zeros_like(band_stack)

    def remote(source, target, sends, recvs, index, device):
        return pltpu.make_async_remote_copy(
            src_ref=source,
            dst_ref=target,
            send_sem=sends.at[index],
            recv_sem=recvs.at[index],
            device_id=device,
            device_id_type=MESH,
        )

    def copies(c, phase):
        order = CHUNKS[c][0]
        t_ref, s_ref, u_ref, r1, r2, r3 = per[6 * c : 6 * c + 6]
        result = []
        for k in (2, 1, 3):
            there, device = peer(order[phase], k)
            if phase == 0:
                source, target = t_ref.at[pl.ds(pl.multiple_of(there * 32, 32), 32)], r1.at[k - 1]
            elif phase == 1:
                source, target = s_ref.at[pl.ds(pl.multiple_of(there * 8, 8), 8)], r2.at[k - 1]
            else:
                source, target = u_ref.at[there], r3.at[k - 1]
            index = (c * 3 + phase) * 3 + k - 1
            result.append(remote(source, target, send_sems, recv_sems, index, device))
        return result

    def low_copies(n, phase):
        order = SETS[n][0]
        l_ref, s_ref, r1, r2 = low_per[4 * n : 4 * n + 4]
        result = []
        for k in (2, 1, 3):
            there, device = peer(order[phase], k)
            if phase == 0:
                source, target = l_ref.at[pl.ds(pl.multiple_of(there * 32, 32), 32)], r1.at[k - 1]
            else:
                source, target = s_ref.at[pl.ds(pl.multiple_of(there * 8, 8), 8)], r2.at[k - 1]
            index = (n * 2 + phase) * 3 + k - 1
            result.append(remote(source, target, low_send, low_recv, index, device))
        return result

    def ring_copies():
        result = []
        for k in (8, 7, 9, 6, 10, 5, 11, 4, 12, 3, 13, 2, 14, 1, 15):
            low, device = ring_peer(k)
            result.append(
                remote(ring_out.at[low], ring_in.at[k - 1], ring_send, ring_recv, k - 1, device)
            )
        return result

    def pair_copy():
        return remote(pair_out, pair_in, pair_send, pair_recv, 0, other)

    def start(batch):
        for copy in batch:
            copy.start()

    def arrive(batch):
        for copy in batch:
            copy.wait_recv()

    def turn(c):
        order, first, width = CHUNKS[c]
        per[6 * c][...] = jnp.dot(
            turned[order], g_ref[:, first : first + width], preferred_element_type=jnp.float32
        )

    def low_first(n):
        order, first, count = SETS[n]
        for j in range(count):
            begin = (first + j) * GROUP
            loads[first + j].wait()
            both = jnp.dot(
                g_ref[:, begin : begin + GROUP], b_ref[...], preferred_element_type=jnp.float32
            )
            high, low = split(both[:, :128] + both[:, 128:])
            low_per[4 * n][:, j * 128 : (j + 1) * 128] = jnp.dot(
                turned[order], high, preferred_element_type=jnp.float32
            ) + jnp.dot(turned[order], low, preferred_element_type=jnp.float32)

    def low_second(n):
        l_ref, s_ref, r1, r2 = low_per[4 * n : 4 * n + 4]
        arrive(low_copies(n, 0))
        own = pl.ds(pl.multiple_of(at[SETS[n][0][0]] * 32, 32), 32)
        s_ref[...] = (l_ref[own, :] + r1[0]) + (r1[1] + r1[2])
        start(low_copies(n, 1))

    def low_third(n):
        l_ref, s_ref, r1, r2 = low_per[4 * n : 4 * n + 4]
        order, first, count = SETS[n]
        arrive(low_copies(n, 1))
        own = pl.ds(pl.multiple_of(at[order[1]] * 8, 8), 8)
        total = (s_ref[own, :] + r2[0]) + (r2[1] + r2[2])
        for q in range(4):
            ring_out[q, :, first * 128 : (first + count) * 128] = total[2 * q : 2 * q + 2]

    def second(c):
        order, first, width = CHUNKS[c]
        t_ref, s_ref, u_ref, r1, r2, r3 = per[6 * c : 6 * c + 6]
        arrive(copies(c, 0))
        own = pl.ds(pl.multiple_of(at[order[0]] * 32, 32), 32)
        s_ref[...] = (t_ref[own, :] + r1[0]) + (r1[1] + r1[2])
        start(copies(c, 1))

    def third(c):
        order, first, width = CHUNKS[c]
        t_ref, s_ref, u_ref, r1, r2, r3 = per[6 * c : 6 * c + 6]
        arrive(copies(c, 1))
        own = pl.ds(pl.multiple_of(at[order[1]] * 8, 8), 8)
        total = (s_ref[own, :] + r2[0]) + (r2[1] + r2[2])
        for q in range(4):
            u_ref[q] = total[2 * q : 2 * q + 2]
        start(copies(c, 2))

    def last(c):
        order, first, width = CHUNKS[c]
        t_ref, s_ref, u_ref, r1, r2, r3 = per[6 * c : 6 * c + 6]
        arrive(copies(c, 2))
        total = (u_ref[at[order[2]]] + r3[0]) + (r3[1] + r3[2])
        blended = DECAY * m_ref[:, first : first + width] + total
        begin = first
        while begin < first + width:
            g = begin // GROUP
            end = min(first + width, (g + 1) * GROUP)
            stack[2 * g : 2 * g + 2, begin - g * GROUP : end - g * GROUP] = blended[
                :, begin - first : end - first
            ]
            begin = end

    def low_fourth():
        arrive(ring_copies())
        terms = [ring_out[at["z"]]] + [ring_in[k] for k in range(RING - 1)]
        while len(terms) > 1:
            terms = [terms[j] + terms[j + 1] for j in range(0, len(terms), 2)]
        pair_out[...] = terms[0]
        pair_copy().start()

    def relay_signal(j):
        for k in (3, 13):
            pl.semaphore_signal(
                relay.at[j], inc=1, device_id=ring_peer(k)[1], device_id_type=MESH
            )

    b_load.wait()
    for n in range(len(SETS)):
        low_first(n)
    for c in range(3):
        turn(c)
    pl.semaphore_wait(barrier, len(greeted))
    relay_signal(0)
    for n in range(len(SETS)):
        start(low_copies(n, 0))
    for c in range(3):
        start(copies(c, 0))
    m_load.wait()
    high, low = b_ref[:, :128], b_ref[:, 128:]
    old = DECAY * m_ref[...]
    for g in range(GROUPS):
        stack[2 * g : 2 * g + 2, :] = old[:, g * GROUP : (g + 1) * GROUP]
    old_band = analyse(stack[...], high, low)
    for g in range(GROUPS):
        old_ref[:, g * 128 : (g + 1) * 128] = old_band[2 * g : 2 * g + 2]
    for c in range(3, N_CHUNKS):
        turn(c)
    for n in range(len(SETS)):
        low_second(n)
    for c in (3, 4):
        start(copies(c, 0))
    pl.semaphore_wait(relay.at[0], 2)
    relay_signal(1)
    second(0)
    second(1)
    for c in (5, 6):
        start(copies(c, 0))
    for n in range(len(SETS)):
        low_third(n)
    ring_out[at["z"]] = ring_out[at["z"]] + old_ref[...]
    pl.semaphore_wait(relay.at[1], 2)
    start(ring_copies())
    second(2)
    second(3)
    second(4)
    third(0)
    third(1)
    third(2)
    second(5)
    second(6)
    third(3)
    third(4)
    last(0)
    last(1)
    last(2)
    third(5)
    third(6)
    low_fourth()
    last(3)
    last(4)
    arrive([pair_copy()])
    for g in range(GROUPS):
        lanes = slice(g * 128, (g + 1) * 128)
        band_stack[2 * g : 2 * g + 2, :] = pair_out[:, lanes] + pair_in[:, lanes]
    update = expand(band_stack[...] * (1.0 / REPS), high, low)
    for g in range(GROUPS):
        update_ref[:, g * GROUP : (g + 1) * GROUP] = update[2 * g : 2 * g + 2]
    last(5)
    last(6)
    blended = stack[...]
    fresh = blended - expand(analyse(blended, high, low), high, low)
    for g in range(GROUPS):
        fresh_ref[0, :, g * GROUP : (g + 1) * GROUP] = fresh[2 * g : 2 * g + 2]
    sent = [copy for c in range(N_CHUNKS) for phase in range(3) for copy in copies(c, phase)]
    sent += [copy for n in range(len(SETS)) for phase in range(2) for copy in low_copies(n, phase)]
    sent += ring_copies() + [pair_copy()]
    for copy in sent:
        copy.wait_send()


def shards(gradients, momentum):
    basis = jnp.asarray(halves())
    f32 = jnp.float32
    per = []
    for order, first, width in CHUNKS:
        per += [
            pltpu.VMEM((ROWS, width), f32),
            pltpu.VMEM((32, width), f32),
            pltpu.VMEM((4, 2, width), f32),
            pltpu.VMEM((3, 32, width), f32),
            pltpu.VMEM((3, 8, width), f32),
            pltpu.VMEM((3, 2, width), f32),
        ]
    low_per = []
    for order, first, count in SETS:
        width = count * 128
        low_per += [
            pltpu.VMEM((ROWS, width), f32),
            pltpu.VMEM((32, width), f32),
            pltpu.VMEM((3, 32, width), f32),
            pltpu.VMEM((3, 8, width), f32),
        ]
    return pl.pallas_call(
        kernel,
        out_shape=(
            jax.ShapeDtypeStruct((1, 2, D), f32),
            jax.ShapeDtypeStruct((2, D), f32),
        ),
        in_specs=[pl.BlockSpec(memory_space=pltpu.HBM)] * 3,
        out_specs=(pl.BlockSpec(memory_space=pltpu.VMEM),) * 2,
        scratch_shapes=[
            pltpu.VMEM((ROWS, D), jnp.bfloat16),
            pltpu.VMEM((2, D), f32),
            pltpu.VMEM((GROUP, 256), jnp.bfloat16),
            pltpu.VMEM((16, GROUP), f32),
            pltpu.VMEM((16, 128), f32),
            *per,
            *low_per,
            pltpu.VMEM((4, 2, BANDS), f32),
            pltpu.VMEM((RING - 1, 2, BANDS), f32),
            pltpu.VMEM((2, BANDS), f32),
            pltpu.VMEM((2, BANDS), f32),
            pltpu.VMEM((2, BANDS), f32),
            pltpu.SemaphoreType.DMA((GROUPS + 2,)),
            pltpu.SemaphoreType.DMA((9 * N_CHUNKS,)),
            pltpu.SemaphoreType.DMA((9 * N_CHUNKS,)),
            pltpu.SemaphoreType.DMA((6 * len(SETS),)),
            pltpu.SemaphoreType.DMA((6 * len(SETS),)),
            pltpu.SemaphoreType.DMA((RING - 1,)),
            pltpu.SemaphoreType.DMA((RING - 1,)),
            pltpu.SemaphoreType.DMA((1,)),
            pltpu.SemaphoreType.DMA((1,)),
            pltpu.SemaphoreType.REGULAR((2,)),
        ],
        compiler_params=pltpu.CompilerParams(
            collective_id=0, has_side_effects=True, vmem_limit_bytes=48 << 20
        ),
        name="momentum_step",
    )(gradients, momentum, basis)


def solution(mesh):
    return jax.shard_map(
        shards,
        mesh=mesh,
        in_specs=(P("rep", "fsdp", None, None), P("rep", "fsdp", None)),
        out_specs=(P("rep", "fsdp", None), P("fsdp", None)),
        check_vma=False,
    )
```

```python
import jax
import jax.numpy as jnp
import ml_dtypes
import numpy as np
from jax import lax
from jax.experimental import pallas as pl
from jax.experimental.pallas import tpu as pltpu
from jax.sharding import PartitionSpec as P

SPAN = 64
BAND = 8
D = 5120
ROWS = 128
GROUP = 1024
GROUPS = D // GROUP
DECAY = 0.9
MESH = pl.DeviceIdType.MESH

REPS = 8
RING = 16

CHUNKS = (
    ("xyz", 0, 896),
    ("yxz", 896, 896),
    ("zxy", 1792, 512),
    ("xyz", 2304, 512),
    ("yxz", 2816, 512),
    ("xyz", 3328, 896),
    ("yxz", 4224, 896),
)
N_CHUNKS = len(CHUNKS)
SETS = (("xyz", 0, 2), ("yxz", 2, 3))
BANDS = D // SPAN * BAND


def halves():
    freq = np.arange(BAND)[:, None]
    place = np.arange(SPAN)[None, :]
    table = np.cos(np.pi * (2.0 * place + 1.0) * freq / (2.0 * SPAN)) * np.sqrt(2.0 / SPAN)
    table = table * np.where(freq == 0, np.sqrt(0.5), 1.0)
    full = np.zeros((GROUP, GROUP // SPAN * BAND), np.float32)
    for block in range(GROUP // SPAN):
        full[block * SPAN : (block + 1) * SPAN, block * BAND : (block + 1) * BAND] = table.T
    high = full.astype(ml_dtypes.bfloat16)
    low = (full - high.astype(np.float32)).astype(ml_dtypes.bfloat16)
    return np.concatenate([high, low], axis=1)


def half(width):
    return (width // 128 + 1) // 2 * 128


def selector(source):
    column = lax.broadcasted_iota(jnp.int32, (ROWS, ROWS), 1)
    return jnp.where(source == column, 1.0, 0.0).astype(jnp.bfloat16)


WEIGHT = {"y": 32, "z": 8, "x": 2}


def permutation(order):
    row = lax.broadcasted_iota(jnp.int32, (ROWS, ROWS), 0)
    return selector(
        ((row >> 5) & 3) * WEIGHT[order[0]]
        + ((row >> 3) & 3) * WEIGHT[order[1]]
        + ((row >> 1) & 3) * WEIGHT[order[2]]
        + (row & 1)
    )


def band_permutation(order):
    row = lax.broadcasted_iota(jnp.int32, (ROWS, ROWS), 0)
    return selector(
        ((row >> 4) & 3) * WEIGHT[order[0]]
        + ((row >> 2) & 3) * WEIGHT[order[1]]
        + (row & 3) * WEIGHT[order[2]]
        + (row >> 6)
    )


def split(value):
    high = value.astype(jnp.bfloat16)
    return high, (value - high.astype(jnp.float32)).astype(jnp.bfloat16)


def analyse(value, basis_high, basis_low):
    high, low = split(value)
    dims = (((1,), (0,)), ((), ()))
    f32 = jnp.float32
    return (
        lax.dot_general(high, basis_high, dims, preferred_element_type=f32)
        + lax.dot_general(high, basis_low, dims, preferred_element_type=f32)
        + lax.dot_general(low, basis_high, dims, preferred_element_type=f32)
    )


def expand(value, basis_high, basis_low):
    high, low = split(value)
    dims = (((1,), (1,)), ((), ()))
    f32 = jnp.float32
    return (
        lax.dot_general(high, basis_high, dims, preferred_element_type=f32)
        + lax.dot_general(high, basis_low, dims, preferred_element_type=f32)
        + lax.dot_general(low, basis_high, dims, preferred_element_type=f32)
    )


def kernel(g_hbm, m_hbm, b_hbm, fresh_ref, update_ref, *scratch):
    scratch = list(scratch)
    take = lambda n: [scratch.pop(0) for _ in range(n)]
    g_ref, m_ref, b_ref, stack, band_stack = take(5)
    per = take(8 * N_CHUNKS)
    low_per = take(6 * len(SETS))
    ring_out, ring_in, pair_out, pair_in, old_ref, old_in = take(6)
    load_sems, send_sems, recv_sems, low_send, low_recv = take(5)
    ring_send, ring_recv, pair_send, pair_recv, relay = take(5)

    rep = lax.axis_index("rep")
    fsdp = lax.axis_index("fsdp")
    core = rep % 2
    at = {"y": fsdp // 16, "z": (fsdp // 4) % 4, "x": fsdp % 4}
    stride = {"y": 16, "z": 4, "x": 1}
    height = (rep // 2) * 4 + at["z"]

    def peer(axis, k):
        there = lax.rem(at[axis] + k, 4)
        return there, {"rep": rep, "fsdp": fsdp + (there - at[axis]) * stride[axis]}

    def ring_peer(k):
        there = lax.rem(height + k, RING)
        low = there % 4
        return low, {"rep": (there // 4) * 2 + core, "fsdp": fsdp + (low - at["z"]) * 4}

    other = {"rep": rep + 1 - 2 * core, "fsdp": fsdp}

    barrier = pltpu.get_barrier_semaphore()
    greeted = [ring_peer(k)[1] for k in (3, 13, 2, 14, 1, 15)]
    greeted += [peer(axis, k)[1] for k in (2, 1, 3) for axis in "xy"]
    greeted.append(other)
    for device in greeted:
        pl.semaphore_signal(barrier, inc=1, device_id=device, device_id_type=MESH)

    loads = []
    for g in range(GROUPS):
        columns = pl.ds(g * GROUP, GROUP)
        loads.append(
            pltpu.make_async_copy(g_hbm.at[0, 0, :, columns], g_ref.at[:, columns], load_sems.at[g])
        )
    b_load = pltpu.make_async_copy(b_hbm, b_ref, load_sems.at[GROUPS + 1])
    m_load = pltpu.make_async_copy(m_hbm.at[0], m_ref, load_sems.at[GROUPS])
    b_load.start()
    for load in loads:
        load.start()
    m_load.start()

    turned = {order: permutation(order) for order in ("xyz", "yxz", "zxy")}
    stack[...] = jnp.zeros_like(stack)
    band_stack[...] = jnp.zeros_like(band_stack)

    def remote(source, target, sends, recvs, index, device):
        return pltpu.make_async_remote_copy(
            src_ref=source,
            dst_ref=target,
            send_sem=sends.at[index],
            recv_sem=recvs.at[index],
            device_id=device,
            device_id_type=MESH,
        )

    def rows(place, count):
        return pl.ds(pl.multiple_of(place * count, count), count)

    def copies(c, phase):
        order, first, width = CHUNKS[c]
        t_ref, s_ref, u_ref, r1, r2, r3, ra, rb = per[8 * c : 8 * c + 8]
        result = []
        for k in (2, 1, 3):
            there, device = peer(order[phase], k)
            if phase == 0:
                source, target = t_ref.at[rows(there, 32)], r1.at[k - 1]
            elif phase == 1:
                source, target = s_ref.at[rows(there, 8)], r2.at[k - 1]
            else:
                source, target = u_ref.at[there], r3.at[k - 1]
            index = c * 12 + (phase * 3 + 3 if phase else 0) + k - 1
            result.append(remote(source, target, send_sems, recv_sems, index, device))
        return result

    def hops(c, step, begin=0, end=4):
        order, first, width = CHUNKS[c]
        t_ref, s_ref, u_ref, r1, r2, r3, ra, rb = per[8 * c : 8 * c + 8]
        cut = half(width)
        one, two = pl.ds(0, cut), pl.ds(cut, width - cut)
        far = peer(order[0], 2)[0]
        after, up = peer(order[0], 1)
        before, down = peer(order[0], 3)
        if step == 0:
            moves = [
                (t_ref.at[rows(far, 32), one], ra, up),
                (t_ref.at[rows(far, 32), two], rb, down),
                (t_ref.at[rows(after, 32), two], r1.at[0, :, two], up),
                (t_ref.at[rows(before, 32), one], r1.at[1, :, one], down),
            ]
        else:
            moves = [
                (t_ref.at[rows(after, 32), one], r1.at[0, :, one], up),
                (t_ref.at[rows(before, 32), two], r1.at[1, :, two], down),
            ]
        return [
            remote(source, target, send_sems, recv_sems, c * 12 + step * 4 + j, device)
            for j, (source, target, device) in enumerate(moves)
            if begin <= j < end
        ]

    def low_copies(n, phase):
        order = SETS[n][0]
        l_ref, k_ref, v_ref, s_ref, r1, r2 = low_per[6 * n : 6 * n + 6]
        result = []
        for k in (2, 1, 3):
            there, device = peer(order[phase], k)
            if phase == 0:
                source, target = v_ref.at[rows(there, 16)], r1.at[k - 1]
            else:
                source, target = s_ref.at[there], r2.at[k - 1]
            index = (n * 2 + phase) * 3 + k - 1
            result.append(remote(source, target, low_send, low_recv, index, device))
        return result

    def swap_copy(n):
        l_ref, k_ref = low_per[6 * n : 6 * n + 2]
        return remote(l_ref.at[rows(1 - core, 64)], k_ref, pair_send, pair_recv, n + 1, other)

    def ring_copies():
        result = []
        for k in (8, 7, 9, 6, 10, 5, 11, 4, 12, 3, 13, 2, 14, 1, 15):
            low, device = ring_peer(k)
            result.append(
                remote(ring_out.at[low], ring_in.at[k - 1], ring_send, ring_recv, k - 1, device)
            )
        return result

    def old_copy():
        return remote(old_ref.at[1 - core], old_in, pair_send, pair_recv, len(SETS) + 1, other)

    def pair_copy():
        return remote(pair_out, pair_in, pair_send, pair_recv, 0, other)

    def start(batch):
        for copy in batch:
            copy.start()

    def arrive(batch):
        for copy in batch:
            copy.wait_recv()

    def turn(c):
        order, first, width = CHUNKS[c]
        per[8 * c][...] = jnp.dot(
            turned[order], g_ref[:, first : first + width], preferred_element_type=jnp.float32
        )

    def low_first(n):
        order, first, count = SETS[n]
        place = band_permutation(order)
        for j in range(count):
            begin = (first + j) * GROUP
            both = jnp.dot(
                g_ref[:, begin : begin + GROUP], b_ref[...], preferred_element_type=jnp.float32
            )
            high, low = split(both[:, :128] + both[:, 128:])
            low_per[6 * n][:, j * 128 : (j + 1) * 128] = jnp.dot(
                place, high, preferred_element_type=jnp.float32
            ) + jnp.dot(place, low, preferred_element_type=jnp.float32)
        swap_copy(n).start()

    def low_swapped(n):
        l_ref, k_ref, v_ref, s_ref, r1, r2 = low_per[6 * n : 6 * n + 6]
        arrive([swap_copy(n)])
        v_ref[...] = l_ref[rows(core, 64), :] + k_ref[...]
        start(low_copies(n, 0))

    def low_second(n):
        l_ref, k_ref, v_ref, s_ref, r1, r2 = low_per[6 * n : 6 * n + 6]
        arrive(low_copies(n, 0))
        total = (v_ref[rows(at[SETS[n][0][0]], 16), :] + r1[0]) + (r1[1] + r1[2])
        for q in range(4):
            s_ref[q] = total[4 * q : 4 * q + 4]
        start(low_copies(n, 1))

    def low_third(n):
        l_ref, k_ref, v_ref, s_ref, r1, r2 = low_per[6 * n : 6 * n + 6]
        order, first, count = SETS[n]
        arrive(low_copies(n, 1))
        total = (s_ref[at[order[1]]] + r2[0]) + (r2[1] + r2[2])
        for q in range(4):
            ring_out[q, :, first * 128 : (first + count) * 128] = total[q : q + 1]

    def relayed(c):
        order, first, width = CHUNKS[c]
        t_ref, s_ref, u_ref, r1, r2, r3, ra, rb = per[8 * c : 8 * c + 8]
        cut = half(width)
        arrive(hops(c, 0, 0, 2))
        after, before = rows(peer(order[0], 1)[0], 32), rows(peer(order[0], 3)[0], 32)
        t_ref[after, :cut] = t_ref[after, :cut] + ra[...]
        t_ref[before, cut:] = t_ref[before, cut:] + rb[...]
        start(hops(c, 1))

    def second(c):
        order, first, width = CHUNKS[c]
        t_ref, s_ref, u_ref, r1, r2, r3, ra, rb = per[8 * c : 8 * c + 8]
        own = rows(at[order[0]], 32)
        if order[0] == "z":
            arrive(copies(c, 0))
            s_ref[...] = (t_ref[own, :] + r1[0]) + (r1[1] + r1[2])
        else:
            arrive(hops(c, 0, 2) + hops(c, 1))
            s_ref[...] = t_ref[own, :] + (r1[0] + r1[1])
        start(copies(c, 1))

    def third(c):
        order, first, width = CHUNKS[c]
        t_ref, s_ref, u_ref, r1, r2, r3, ra, rb = per[8 * c : 8 * c + 8]
        arrive(copies(c, 1))
        own = pl.ds(pl.multiple_of(at[order[1]] * 8, 8), 8)
        total = (s_ref[own, :] + r2[0]) + (r2[1] + r2[2])
        for q in range(4):
            u_ref[q] = total[2 * q : 2 * q + 2]
        start(copies(c, 2))

    def last(c):
        order, first, width = CHUNKS[c]
        t_ref, s_ref, u_ref, r1, r2, r3, ra, rb = per[8 * c : 8 * c + 8]
        arrive(copies(c, 2))
        total = (u_ref[at[order[2]]] + r3[0]) + (r3[1] + r3[2])
        blended = DECAY * m_ref[:, first : first + width] + total
        begin = first
        while begin < first + width:
            g = begin // GROUP
            end = min(first + width, (g + 1) * GROUP)
            stack[2 * g : 2 * g + 2, begin - g * GROUP : end - g * GROUP] = blended[
                :, begin - first : end - first
            ]
            begin = end

    def low_fourth():
        arrive(ring_copies())
        terms = [ring_out[at["z"]]] + [ring_in[k] for k in range(RING - 1)]
        while len(terms) > 1:
            terms = [terms[j] + terms[j + 1] for j in range(0, len(terms), 2)]
        pair_out[...] = terms[0]
        pair_copy().start()

    def relay_signal(j):
        for k in (3, 13):
            pl.semaphore_signal(
                relay.at[j], inc=1, device_id=ring_peer(k)[1], device_id_type=MESH
            )

    loads[0].wait()
    turn(0)
    pl.semaphore_wait(barrier, len(greeted))
    relay_signal(0)
    start(hops(0, 0))
    loads[1].wait()
    turn(1)
    start(hops(1, 0))
    loads[2].wait()
    turn(2)
    start(copies(2, 0))
    b_load.wait()
    low_first(0)
    loads[3].wait()
    loads[4].wait()
    low_first(1)
    low_swapped(0)
    low_swapped(1)
    for c in range(3, N_CHUNKS):
        turn(c)
    m_load.wait()
    high, low = b_ref[:, :128], b_ref[:, 128:]
    old = DECAY * m_ref[...]
    for g in range(GROUPS):
        stack[2 * g : 2 * g + 2, :] = old[:, g * GROUP : (g + 1) * GROUP]
    old_band = analyse(stack[...], high, low)
    for g in range(GROUPS):
        for i in range(2):
            old_ref[i, :, g * 128 : (g + 1) * 128] = old_band[2 * g + i : 2 * g + i + 1]
    start([old_copy()])
    pl.semaphore_wait(relay.at[0], 2)
    relay_signal(1)
    relayed(0)
    relayed(1)
    start(hops(3, 0))
    start(hops(4, 0))
    for n in range(len(SETS)):
        low_second(n)
    start(hops(5, 0))
    start(hops(6, 0))
    relayed(3)
    relayed(4)
    for n in range(len(SETS)):
        low_third(n)
    arrive([old_copy()])
    ring_out[at["z"]] = ring_out[at["z"]] + (old_ref[core] + old_in[...])
    pl.semaphore_wait(relay.at[1], 2)
    start(ring_copies())
    second(0)
    second(1)
    second(2)
    relayed(5)
    relayed(6)
    third(0)
    third(1)
    second(3)
    second(4)
    third(2)
    second(5)
    second(6)
    last(0)
    last(1)
    third(3)
    third(4)
    last(2)
    low_fourth()
    third(5)
    third(6)
    last(3)
    last(4)
    arrive([pair_copy()])
    for g in range(GROUPS):
        lanes = slice(g * 128, (g + 1) * 128)
        mine, theirs = pair_out[:, lanes], pair_in[:, lanes]
        band_stack[2 * g : 2 * g + 1, :] = jnp.where(core == 0, mine, theirs)
        band_stack[2 * g + 1 : 2 * g + 2, :] = jnp.where(core == 0, theirs, mine)
    update = expand(band_stack[...] * (1.0 / REPS), high, low)
    for g in range(GROUPS):
        update_ref[:, g * GROUP : (g + 1) * GROUP] = update[2 * g : 2 * g + 2]
    last(5)
    last(6)
    blended = stack[...]
    fresh = blended - expand(analyse(blended, high, low), high, low)
    for g in range(GROUPS):
        fresh_ref[0, :, g * GROUP : (g + 1) * GROUP] = fresh[2 * g : 2 * g + 2]
    sent = []
    for c in range(N_CHUNKS):
        sent += copies(c, 0) if CHUNKS[c][0][0] == "z" else hops(c, 0) + hops(c, 1)
        sent += copies(c, 1) + copies(c, 2)
    sent += [copy for n in range(len(SETS)) for phase in range(2) for copy in low_copies(n, phase)]
    sent += ring_copies() + [pair_copy(), old_copy()] + [swap_copy(n) for n in range(len(SETS))]
    for copy in sent:
        copy.wait_send()


def shards(gradients, momentum):
    basis = jnp.asarray(halves())
    f32 = jnp.float32
    per = []
    for order, first, width in CHUNKS:
        per += [
            pltpu.VMEM((ROWS, width), f32),
            pltpu.VMEM((32, width), f32),
            pltpu.VMEM((4, 2, width), f32),
            pltpu.VMEM((3 if order[0] == "z" else 2, 32, width), f32),
            pltpu.VMEM((3, 8, width), f32),
            pltpu.VMEM((3, 2, width), f32),
            pltpu.VMEM((32, half(width)), f32),
            pltpu.VMEM((32, width - half(width)), f32),
        ]
    low_per = []
    for order, first, count in SETS:
        width = count * 128
        low_per += [
            pltpu.VMEM((ROWS, width), f32),
            pltpu.VMEM((64, width), f32),
            pltpu.VMEM((64, width), f32),
            pltpu.VMEM((4, 4, width), f32),
            pltpu.VMEM((3, 16, width), f32),
            pltpu.VMEM((3, 4, width), f32),
        ]
    return pl.pallas_call(
        kernel,
        out_shape=(
            jax.ShapeDtypeStruct((1, 2, D), f32),
            jax.ShapeDtypeStruct((2, D), f32),
        ),
        in_specs=[pl.BlockSpec(memory_space=pltpu.HBM)] * 3,
        out_specs=(pl.BlockSpec(memory_space=pltpu.VMEM),) * 2,
        scratch_shapes=[
            pltpu.VMEM((ROWS, D), jnp.bfloat16),
            pltpu.VMEM((2, D), f32),
            pltpu.VMEM((GROUP, 256), jnp.bfloat16),
            pltpu.VMEM((16, GROUP), f32),
            pltpu.VMEM((16, 128), f32),
            *per,
            *low_per,
            pltpu.VMEM((4, 1, BANDS), f32),
            pltpu.VMEM((RING - 1, 1, BANDS), f32),
            pltpu.VMEM((1, BANDS), f32),
            pltpu.VMEM((1, BANDS), f32),
            pltpu.VMEM((2, 1, BANDS), f32),
            pltpu.VMEM((1, BANDS), f32),
            pltpu.SemaphoreType.DMA((GROUPS + 2,)),
            pltpu.SemaphoreType.DMA((12 * N_CHUNKS,)),
            pltpu.SemaphoreType.DMA((12 * N_CHUNKS,)),
            pltpu.SemaphoreType.DMA((6 * len(SETS),)),
            pltpu.SemaphoreType.DMA((6 * len(SETS),)),
            pltpu.SemaphoreType.DMA((RING - 1,)),
            pltpu.SemaphoreType.DMA((RING - 1,)),
            pltpu.SemaphoreType.DMA((len(SETS) + 2,)),
            pltpu.SemaphoreType.DMA((len(SETS) + 2,)),
            pltpu.SemaphoreType.REGULAR((2,)),
        ],
        compiler_params=pltpu.CompilerParams(
            collective_id=0, has_side_effects=True, vmem_limit_bytes=107 << 19
        ),
        name="momentum_step",
    )(gradients, momentum, basis)


def solution(mesh):
    return jax.shard_map(
        shards,
        mesh=mesh,
        in_specs=(P("rep", "fsdp", None, None), P("rep", "fsdp", None)),
        out_specs=(P("rep", "fsdp", None), P("fsdp", None)),
        check_vma=False,
    )
```

```python
import jax
import jax.numpy as jnp
import ml_dtypes
import numpy as np
from jax import lax
from jax.experimental import pallas as pl
from jax.experimental.pallas import tpu as pltpu
from jax.sharding import PartitionSpec as P

SPAN = 64
BAND = 8
D = 5120
ROWS = 128
GROUP = 1024
GROUPS = D // GROUP
DECAY = 0.9
MESH = pl.DeviceIdType.MESH

REPS = 8
RING = 16

CHUNKS = (
    ("xyz", 0, 896),
    ("yxz", 896, 896),
    ("zxy", 1792, 512),
    ("xyz", 2304, 896),
    ("yxz", 3200, 896),
    ("xyz", 4096, 512),
    ("yxz", 4608, 512),
)
N_CHUNKS = len(CHUNKS)
SETS = (("xyz", 0, 2), ("yxz", 2, 3))
BANDS = D // SPAN * BAND


def halves():
    freq = np.arange(BAND)[:, None]
    place = np.arange(SPAN)[None, :]
    table = np.cos(np.pi * (2.0 * place + 1.0) * freq / (2.0 * SPAN)) * np.sqrt(2.0 / SPAN)
    table = table * np.where(freq == 0, np.sqrt(0.5), 1.0)
    full = np.zeros((GROUP, GROUP // SPAN * BAND), np.float32)
    for block in range(GROUP // SPAN):
        full[block * SPAN : (block + 1) * SPAN, block * BAND : (block + 1) * BAND] = table.T
    high = full.astype(ml_dtypes.bfloat16)
    low = (full - high.astype(np.float32)).astype(ml_dtypes.bfloat16)
    return np.concatenate([high, low], axis=1)


def half(width):
    return (width // 128 + 1) // 2 * 128


def selector(source):
    column = lax.broadcasted_iota(jnp.int32, (ROWS, ROWS), 1)
    return jnp.where(source == column, 1.0, 0.0).astype(jnp.bfloat16)


WEIGHT = {"y": 32, "z": 8, "x": 2}


def permutation(order):
    row = lax.broadcasted_iota(jnp.int32, (ROWS, ROWS), 0)
    return selector(
        ((row >> 5) & 3) * WEIGHT[order[0]]
        + ((row >> 3) & 3) * WEIGHT[order[1]]
        + ((row >> 1) & 3) * WEIGHT[order[2]]
        + (row & 1)
    )


def band_permutation(order):
    row = lax.broadcasted_iota(jnp.int32, (ROWS, ROWS), 0)
    return selector(
        ((row >> 4) & 3) * WEIGHT[order[0]]
        + ((row >> 2) & 3) * WEIGHT[order[1]]
        + (row & 3) * WEIGHT[order[2]]
        + (row >> 6)
    )


def split(value):
    high = value.astype(jnp.bfloat16)
    return high, (value - high.astype(jnp.float32)).astype(jnp.bfloat16)


def analyse(value, basis_high, basis_low):
    high, low = split(value)
    dims = (((1,), (0,)), ((), ()))
    f32 = jnp.float32
    return (
        lax.dot_general(high, basis_high, dims, preferred_element_type=f32)
        + lax.dot_general(high, basis_low, dims, preferred_element_type=f32)
        + lax.dot_general(low, basis_high, dims, preferred_element_type=f32)
    )


def expand(value, basis_high, basis_low):
    high, low = split(value)
    dims = (((1,), (1,)), ((), ()))
    f32 = jnp.float32
    return (
        lax.dot_general(high, basis_high, dims, preferred_element_type=f32)
        + lax.dot_general(high, basis_low, dims, preferred_element_type=f32)
        + lax.dot_general(low, basis_high, dims, preferred_element_type=f32)
    )


def kernel(g_hbm, m_hbm, b_hbm, fresh_ref, update_ref, *scratch):
    scratch = list(scratch)
    take = lambda n: [scratch.pop(0) for _ in range(n)]
    g_ref, m_ref, b_ref, stack, band_stack = take(5)
    per = take(8 * N_CHUNKS)
    low_per = take(6 * len(SETS))
    ring_out, ring_in, pair_out, pair_in, old_ref, old_in = take(6)
    load_sems, send_sems, recv_sems, low_send, low_recv = take(5)
    ring_send, ring_recv, pair_send, pair_recv, relay = take(5)

    rep = lax.axis_index("rep")
    fsdp = lax.axis_index("fsdp")
    core = rep % 2
    at = {"y": fsdp // 16, "z": (fsdp // 4) % 4, "x": fsdp % 4}
    stride = {"y": 16, "z": 4, "x": 1}
    height = (rep // 2) * 4 + at["z"]

    def peer(axis, k):
        there = lax.rem(at[axis] + k, 4)
        return there, {"rep": rep, "fsdp": fsdp + (there - at[axis]) * stride[axis]}

    def ring_peer(k):
        there = lax.rem(height + k, RING)
        low = there % 4
        return low, {"rep": (there // 4) * 2 + core, "fsdp": fsdp + (low - at["z"]) * 4}

    other = {"rep": rep + 1 - 2 * core, "fsdp": fsdp}

    cube, level = rep // 2, at["z"]
    waits_down, waits_up = cube >= 1, cube == 3
    crossing = [(k, level + k > 3, waits_up, cube < 3) for k in (1, 2, 3)]
    crossing += [(-k, level < k, waits_down, cube == 0) for k in (1, 2, 3)]

    def across(k):
        return ring_peer((k + RING) % RING)[1]

    barrier = pltpu.get_barrier_semaphore()
    for k, crosses, mine, theirs in crossing:

        @pl.when(jnp.logical_and(crosses, theirs))
        def _():
            pl.semaphore_signal(barrier, inc=1, device_id=across(k), device_id_type=MESH)

    for k in (2, 1, 3):
        for axis in "zxy":
            pl.semaphore_signal(barrier, inc=1, device_id=peer(axis, k)[1], device_id_type=MESH)
    pl.semaphore_signal(barrier, inc=1, device_id=other, device_id_type=MESH)
    entry = 10 + jnp.where(waits_down, 3 - level, 0) + jnp.where(waits_up, level, 0)
    greetings = jnp.where(waits_down, 0, 3 - level) + jnp.where(waits_up, 0, level)

    loads = []
    for g in range(GROUPS):
        columns = pl.ds(g * GROUP, GROUP)
        loads.append(
            pltpu.make_async_copy(g_hbm.at[0, 0, :, columns], g_ref.at[:, columns], load_sems.at[g])
        )
    b_load = pltpu.make_async_copy(b_hbm, b_ref, load_sems.at[GROUPS + 1])
    m_load = pltpu.make_async_copy(m_hbm.at[0], m_ref, load_sems.at[GROUPS])
    b_load.start()
    for load in loads:
        load.start()
    m_load.start()

    turned = {order: permutation(order) for order in ("xyz", "yxz", "zxy")}
    stack[...] = jnp.zeros_like(stack)
    band_stack[...] = jnp.zeros_like(band_stack)

    def remote(source, target, sends, recvs, index, device):
        return pltpu.make_async_remote_copy(
            src_ref=source,
            dst_ref=target,
            send_sem=sends.at[index],
            recv_sem=recvs.at[index],
            device_id=device,
            device_id_type=MESH,
        )

    def rows(place, count):
        return pl.ds(pl.multiple_of(place * count, count), count)

    def copies(c, phase):
        order, first, width = CHUNKS[c]
        t_ref, s_ref, u_ref, r1, r2, r3, ra, rb = per[8 * c : 8 * c + 8]
        result = []
        for k in (2, 1, 3):
            there, device = peer(order[phase], k)
            if phase == 0:
                source, target = t_ref.at[rows(there, 32)], r1.at[k - 1]
            elif phase == 1:
                source, target = s_ref.at[rows(there, 8)], r2.at[k - 1]
            else:
                source, target = u_ref.at[there], r3.at[k - 1]
            index = c * 12 + (phase * 3 + 3 if phase else 0) + k - 1
            result.append(remote(source, target, send_sems, recv_sems, index, device))
        return result

    def hops(c, step, begin=0, end=4):
        order, first, width = CHUNKS[c]
        t_ref, s_ref, u_ref, r1, r2, r3, ra, rb = per[8 * c : 8 * c + 8]
        cut = half(width)
        one, two = pl.ds(0, cut), pl.ds(cut, width - cut)
        far = peer(order[0], 2)[0]
        after, up = peer(order[0], 1)
        before, down = peer(order[0], 3)
        if step == 0:
            moves = [
                (t_ref.at[rows(far, 32), one], ra, up),
                (t_ref.at[rows(far, 32), two], rb, down),
                (t_ref.at[rows(after, 32), two], r1.at[0, :, two], up),
                (t_ref.at[rows(before, 32), one], r1.at[1, :, one], down),
            ]
        else:
            moves = [
                (t_ref.at[rows(after, 32), one], r1.at[0, :, one], up),
                (t_ref.at[rows(before, 32), two], r1.at[1, :, two], down),
            ]
        return [
            remote(source, target, send_sems, recv_sems, c * 12 + step * 4 + j, device)
            for j, (source, target, device) in enumerate(moves)
            if begin <= j < end
        ]

    def low_copies(n, phase):
        order = SETS[n][0]
        l_ref, k_ref, v_ref, s_ref, r1, r2 = low_per[6 * n : 6 * n + 6]
        result = []
        for k in (2, 1, 3):
            there, device = peer(order[phase], k)
            if phase == 0:
                source, target = v_ref.at[rows(there, 16)], r1.at[k - 1]
            else:
                source, target = s_ref.at[there], r2.at[k - 1]
            index = (n * 2 + phase) * 3 + k - 1
            result.append(remote(source, target, low_send, low_recv, index, device))
        return result

    def swap_copy(n):
        l_ref, k_ref = low_per[6 * n : 6 * n + 2]
        return remote(l_ref.at[rows(1 - core, 64)], k_ref, pair_send, pair_recv, n + 1, other)

    def ring_copies():
        result = []
        for k in (8, 7, 9, 6, 10, 5, 11, 4, 12, 3, 13, 2, 14, 1, 15):
            low, device = ring_peer(k)
            result.append(
                remote(ring_out.at[low], ring_in.at[k - 1], ring_send, ring_recv, k - 1, device)
            )
        return result

    def old_copy():
        return remote(old_ref.at[1 - core], old_in, pair_send, pair_recv, len(SETS) + 1, other)

    def pair_copy():
        return remote(pair_out, pair_in, pair_send, pair_recv, 0, other)

    def start(batch):
        for copy in batch:
            copy.start()

    def arrive(batch):
        for copy in batch:
            copy.wait_recv()

    def turn(c):
        order, first, width = CHUNKS[c]
        per[8 * c][...] = jnp.dot(
            turned[order], g_ref[:, first : first + width], preferred_element_type=jnp.float32
        )

    def low_first(n):
        order, first, count = SETS[n]
        place = band_permutation(order)
        parts = []
        for j in range(count):
            begin = (first + j) * GROUP
            both = jnp.dot(
                g_ref[:, begin : begin + GROUP], b_ref[...], preferred_element_type=jnp.float32
            )
            parts.append(both[:, :128] + both[:, 128:])
        high, low = split(jnp.concatenate(parts, axis=1))
        low_per[6 * n][...] = jnp.dot(place, high, preferred_element_type=jnp.float32) + jnp.dot(
            place, low, preferred_element_type=jnp.float32
        )
        swap_copy(n).start()

    def low_swapped(n):
        l_ref, k_ref, v_ref, s_ref, r1, r2 = low_per[6 * n : 6 * n + 6]
        arrive([swap_copy(n)])
        v_ref[...] = l_ref[rows(core, 64), :] + k_ref[...]
        start(low_copies(n, 0))

    def low_second(n):
        l_ref, k_ref, v_ref, s_ref, r1, r2 = low_per[6 * n : 6 * n + 6]
        arrive(low_copies(n, 0))
        total = (v_ref[rows(at[SETS[n][0][0]], 16), :] + r1[0]) + (r1[1] + r1[2])
        for q in range(4):
            s_ref[q] = total[4 * q : 4 * q + 4]
        start(low_copies(n, 1))

    def low_third(n):
        l_ref, k_ref, v_ref, s_ref, r1, r2 = low_per[6 * n : 6 * n + 6]
        order, first, count = SETS[n]
        arrive(low_copies(n, 1))
        total = (s_ref[at[order[1]]] + r2[0]) + (r2[1] + r2[2])
        for q in range(4):
            ring_out[q, :, first * 128 : (first + count) * 128] = total[q : q + 1]

    def relayed(c):
        order, first, width = CHUNKS[c]
        t_ref, s_ref, u_ref, r1, r2, r3, ra, rb = per[8 * c : 8 * c + 8]
        cut = half(width)
        arrive(hops(c, 0, 0, 2))
        after, before = rows(peer(order[0], 1)[0], 32), rows(peer(order[0], 3)[0], 32)
        t_ref[after, :cut] = t_ref[after, :cut] + ra[...]
        t_ref[before, cut:] = t_ref[before, cut:] + rb[...]
        start(hops(c, 1))

    def second(c):
        order, first, width = CHUNKS[c]
        t_ref, s_ref, u_ref, r1, r2, r3, ra, rb = per[8 * c : 8 * c + 8]
        own = rows(at[order[0]], 32)
        if order[0] == "z":
            arrive(copies(c, 0))
            s_ref[...] = (t_ref[own, :] + r1[0]) + (r1[1] + r1[2])
        else:
            arrive(hops(c, 0, 2) + hops(c, 1))
            s_ref[...] = t_ref[own, :] + (r1[0] + r1[1])
        start(copies(c, 1))

    def third(c):
        order, first, width = CHUNKS[c]
        t_ref, s_ref, u_ref, r1, r2, r3, ra, rb = per[8 * c : 8 * c + 8]
        arrive(copies(c, 1))
        own = pl.ds(pl.multiple_of(at[order[1]] * 8, 8), 8)
        total = (s_ref[own, :] + r2[0]) + (r2[1] + r2[2])
        for q in range(4):
            u_ref[q] = total[2 * q : 2 * q + 2]
        start(copies(c, 2))

    def last(c):
        order, first, width = CHUNKS[c]
        t_ref, s_ref, u_ref, r1, r2, r3, ra, rb = per[8 * c : 8 * c + 8]
        arrive(copies(c, 2))
        total = (u_ref[at[order[2]]] + r3[0]) + (r3[1] + r3[2])
        blended = DECAY * m_ref[:, first : first + width] + total
        begin = first
        while begin < first + width:
            g = begin // GROUP
            end = min(first + width, (g + 1) * GROUP)
            stack[2 * g : 2 * g + 2, begin - g * GROUP : end - g * GROUP] = blended[
                :, begin - first : end - first
            ]
            begin = end

    def low_fourth():
        arrive(ring_copies())
        terms = [ring_out[at["z"]]] + [ring_in[k] for k in range(RING - 1)]
        while len(terms) > 1:
            terms = [terms[j] + terms[j + 1] for j in range(0, len(terms), 2)]
        pair_out[...] = terms[0]
        pair_copy().start()

    def relay_signal(j):
        for k in (3, 13):
            pl.semaphore_signal(
                relay.at[j], inc=1, device_id=ring_peer(k)[1], device_id_type=MESH
            )

    def greet():
        for k, crosses, mine, theirs in crossing:

            @pl.when(jnp.logical_and(crosses, mine))
            def _():
                pl.semaphore_signal(relay.at[2], inc=1, device_id=across(k), device_id_type=MESH)

    def stage(number, when):
        @pl.when(when)
        def _():
            if number == 0:
                @pl.when(greetings > 0)
                def _():
                    pl.semaphore_wait(relay.at[2], greetings)

                relay_signal(0)
            elif number == 1:
                pl.semaphore_wait(relay.at[0], 2)
                relay_signal(1)
            else:
                pl.semaphore_wait(relay.at[1], 2)
                start(ring_copies())

    early, late = cube > 0, cube == 0
    loads[0].wait()
    turn(0)
    pl.semaphore_wait(barrier, entry)
    greet()
    start(hops(0, 0))
    loads[1].wait()
    turn(1)
    start(hops(1, 0))
    loads[2].wait()
    turn(2)
    start(copies(2, 0))
    b_load.wait()
    low_first(0)
    loads[3].wait()
    loads[4].wait()
    low_first(1)
    low_swapped(0)
    low_swapped(1)
    stage(0, early)
    for c in range(3, N_CHUNKS):
        turn(c)
    m_load.wait()
    high, low = b_ref[:, :128], b_ref[:, 128:]
    old = DECAY * m_ref[...]
    for g in range(GROUPS):
        stack[2 * g : 2 * g + 2, :] = old[:, g * GROUP : (g + 1) * GROUP]
    old_band = analyse(stack[...], high, low)
    for g in range(GROUPS):
        for i in range(2):
            old_ref[i, :, g * 128 : (g + 1) * 128] = old_band[2 * g + i : 2 * g + i + 1]
    start([old_copy()])
    relayed(0)
    relayed(1)
    start(hops(3, 0))
    start(hops(4, 0))
    for n in range(len(SETS)):
        low_second(n)
    stage(1, early)
    start(hops(5, 0))
    start(hops(6, 0))
    relayed(3)
    relayed(4)
    stage(0, late)
    for n in range(len(SETS)):
        low_third(n)
    arrive([old_copy()])
    ring_out[at["z"]] = ring_out[at["z"]] + (old_ref[core] + old_in[...])
    second(0)
    second(1)
    stage(2, early)
    second(2)
    stage(1, late)
    relayed(5)
    relayed(6)
    third(0)
    third(1)
    second(3)
    second(4)
    stage(2, late)
    third(2)
    second(5)
    second(6)
    last(0)
    last(1)
    third(3)
    third(4)
    last(2)
    third(5)
    third(6)
    last(3)
    last(4)
    low_fourth()
    last(5)
    last(6)
    blended = stack[...]
    fresh = blended - expand(analyse(blended, high, low), high, low)
    for g in range(GROUPS):
        fresh_ref[0, :, g * GROUP : (g + 1) * GROUP] = fresh[2 * g : 2 * g + 2]
    arrive([pair_copy()])
    for g in range(GROUPS):
        lanes = slice(g * 128, (g + 1) * 128)
        mine, theirs = pair_out[:, lanes], pair_in[:, lanes]
        band_stack[2 * g : 2 * g + 1, :] = jnp.where(core == 0, mine, theirs)
        band_stack[2 * g + 1 : 2 * g + 2, :] = jnp.where(core == 0, theirs, mine)
    update = expand(band_stack[...] * (1.0 / REPS), high, low)
    for g in range(GROUPS):
        update_ref[:, g * GROUP : (g + 1) * GROUP] = update[2 * g : 2 * g + 2]
    sent = []
    for c in range(N_CHUNKS):
        sent += copies(c, 0) if CHUNKS[c][0][0] == "z" else hops(c, 0) + hops(c, 1)
        sent += copies(c, 1) + copies(c, 2)
    sent += [copy for n in range(len(SETS)) for phase in range(2) for copy in low_copies(n, phase)]
    sent += ring_copies() + [pair_copy(), old_copy()] + [swap_copy(n) for n in range(len(SETS))]
    for copy in sent:
        copy.wait_send()


def shards(gradients, momentum):
    basis = jnp.asarray(halves())
    f32 = jnp.float32
    per = []
    for order, first, width in CHUNKS:
        per += [
            pltpu.VMEM((ROWS, width), f32),
            pltpu.VMEM((32, width), f32),
            pltpu.VMEM((4, 2, width), f32),
            pltpu.VMEM((3 if order[0] == "z" else 2, 32, width), f32),
            pltpu.VMEM((3, 8, width), f32),
            pltpu.VMEM((3, 2, width), f32),
            pltpu.VMEM((32, half(width)), f32),
            pltpu.VMEM((32, width - half(width)), f32),
        ]
    low_per = []
    for order, first, count in SETS:
        width = count * 128
        low_per += [
            pltpu.VMEM((ROWS, width), f32),
            pltpu.VMEM((64, width), f32),
            pltpu.VMEM((64, width), f32),
            pltpu.VMEM((4, 4, width), f32),
            pltpu.VMEM((3, 16, width), f32),
            pltpu.VMEM((3, 4, width), f32),
        ]
    return pl.pallas_call(
        kernel,
        out_shape=(
            jax.ShapeDtypeStruct((1, 2, D), f32),
            jax.ShapeDtypeStruct((2, D), f32),
        ),
        in_specs=[pl.BlockSpec(memory_space=pltpu.HBM)] * 3,
        out_specs=(pl.BlockSpec(memory_space=pltpu.VMEM),) * 2,
        scratch_shapes=[
            pltpu.VMEM((ROWS, D), jnp.bfloat16),
            pltpu.VMEM((2, D), f32),
            pltpu.VMEM((GROUP, 256), jnp.bfloat16),
            pltpu.VMEM((16, GROUP), f32),
            pltpu.VMEM((16, 128), f32),
            *per,
            *low_per,
            pltpu.VMEM((4, 1, BANDS), f32),
            pltpu.VMEM((RING - 1, 1, BANDS), f32),
            pltpu.VMEM((1, BANDS), f32),
            pltpu.VMEM((1, BANDS), f32),
            pltpu.VMEM((2, 1, BANDS), f32),
            pltpu.VMEM((1, BANDS), f32),
            pltpu.SemaphoreType.DMA((GROUPS + 2,)),
            pltpu.SemaphoreType.DMA((12 * N_CHUNKS,)),
            pltpu.SemaphoreType.DMA((12 * N_CHUNKS,)),
            pltpu.SemaphoreType.DMA((6 * len(SETS),)),
            pltpu.SemaphoreType.DMA((6 * len(SETS),)),
            pltpu.SemaphoreType.DMA((RING - 1,)),
            pltpu.SemaphoreType.DMA((RING - 1,)),
            pltpu.SemaphoreType.DMA((len(SETS) + 2,)),
            pltpu.SemaphoreType.DMA((len(SETS) + 2,)),
            pltpu.SemaphoreType.REGULAR((3,)),
        ],
        compiler_params=pltpu.CompilerParams(
            collective_id=0, has_side_effects=True, vmem_limit_bytes=55136 << 10
        ),
        name="momentum_step",
    )(gradients, momentum, basis)


def solution(mesh):
    return jax.shard_map(
        shards,
        mesh=mesh,
        in_specs=(P("rep", "fsdp", None, None), P("rep", "fsdp", None)),
        out_specs=(P("rep", "fsdp", None), P("fsdp", None)),
        check_vma=False,
    )
```

```python
import jax
import jax.numpy as jnp
import ml_dtypes
import numpy as np
from jax import lax
from jax.experimental import pallas as pl
from jax.experimental.pallas import tpu as pltpu
from jax.sharding import PartitionSpec as P

SPAN = 64
BAND = 8
D = 5120
ROWS = 128
GROUP = 1024
GROUPS = D // GROUP
DECAY = 0.9
MESH = pl.DeviceIdType.MESH

REPS = 8
RING = 16

CHUNKS = (
    ("xyz", 0, 896),
    ("yxz", 896, 896),
    ("zxy", 1792, 768),
    ("xyz", 2560, 768),
    ("yxz", 3328, 768),
    ("xyz", 4096, 512),
    ("yxz", 4608, 512),
)
N_CHUNKS = len(CHUNKS)
SETS = (("xyz", 0, 2), ("yxz", 2, 3))
BANDS = D // SPAN * BAND


def halves():
    freq = np.arange(BAND)[:, None]
    place = np.arange(SPAN)[None, :]
    table = np.cos(np.pi * (2.0 * place + 1.0) * freq / (2.0 * SPAN)) * np.sqrt(2.0 / SPAN)
    table = table * np.where(freq == 0, np.sqrt(0.5), 1.0)
    full = np.zeros((GROUP, GROUP // SPAN * BAND), np.float32)
    for block in range(GROUP // SPAN):
        full[block * SPAN : (block + 1) * SPAN, block * BAND : (block + 1) * BAND] = table.T
    high = full.astype(ml_dtypes.bfloat16)
    low = (full - high.astype(np.float32)).astype(ml_dtypes.bfloat16)
    return np.concatenate([high, low], axis=1)


def half(width):
    return (width // 128 + 1) // 2 * 128


def selector(source):
    column = lax.broadcasted_iota(jnp.int32, (ROWS, ROWS), 1)
    return jnp.where(source == column, 1.0, 0.0).astype(jnp.bfloat16)


WEIGHT = {"y": 32, "z": 8, "x": 2}


def permutation(order):
    row = lax.broadcasted_iota(jnp.int32, (ROWS, ROWS), 0)
    return selector(
        ((row >> 5) & 3) * WEIGHT[order[0]]
        + ((row >> 3) & 3) * WEIGHT[order[1]]
        + ((row >> 1) & 3) * WEIGHT[order[2]]
        + (row & 1)
    )


def band_permutation(order):
    row = lax.broadcasted_iota(jnp.int32, (ROWS, ROWS), 0)
    return selector(
        ((row >> 4) & 3) * WEIGHT[order[0]]
        + ((row >> 2) & 3) * WEIGHT[order[1]]
        + (row & 3) * WEIGHT[order[2]]
        + (row >> 6)
    )


def split(value):
    high = value.astype(jnp.bfloat16)
    return high, (value - high.astype(jnp.float32)).astype(jnp.bfloat16)


def analyse(value, basis_high, basis_low):
    high, low = split(value)
    dims = (((1,), (0,)), ((), ()))
    f32 = jnp.float32
    return (
        lax.dot_general(high, basis_high, dims, preferred_element_type=f32)
        + lax.dot_general(high, basis_low, dims, preferred_element_type=f32)
        + lax.dot_general(low, basis_high, dims, preferred_element_type=f32)
    )


def expand(value, basis_high, basis_low):
    high, low = split(value)
    dims = (((1,), (1,)), ((), ()))
    f32 = jnp.float32
    return (
        lax.dot_general(high, basis_high, dims, preferred_element_type=f32)
        + lax.dot_general(high, basis_low, dims, preferred_element_type=f32)
        + lax.dot_general(low, basis_high, dims, preferred_element_type=f32)
    )


def kernel(g_hbm, m_hbm, b_hbm, fresh_ref, update_ref, *scratch):
    scratch = list(scratch)
    take = lambda n: [scratch.pop(0) for _ in range(n)]
    g_ref, m_ref, b_ref, stack, band_stack = take(5)
    per = take(8 * N_CHUNKS)
    low_per = take(6 * len(SETS))
    ring_out, ring_in, pair_out, pair_in, old_ref, old_in = take(6)
    load_sems, send_sems, recv_sems, low_send, low_recv = take(5)
    ring_send, ring_recv, pair_send, pair_recv, relay = take(5)

    rep = lax.axis_index("rep")
    fsdp = lax.axis_index("fsdp")
    core = rep % 2
    at = {"y": fsdp // 16, "z": (fsdp // 4) % 4, "x": fsdp % 4}
    stride = {"y": 16, "z": 4, "x": 1}
    height = (rep // 2) * 4 + at["z"]

    def peer(axis, k):
        there = lax.rem(at[axis] + k, 4)
        return there, {"rep": rep, "fsdp": fsdp + (there - at[axis]) * stride[axis]}

    def ring_peer(k):
        there = lax.rem(height + k, RING)
        low = there % 4
        return low, {"rep": (there // 4) * 2 + core, "fsdp": fsdp + (low - at["z"]) * 4}

    other = {"rep": rep + 1 - 2 * core, "fsdp": fsdp}

    cube, level = rep // 2, at["z"]
    waits_down, waits_up = cube >= 1, cube == 3
    crossing = [(k, level + k > 3, waits_up, cube < 3) for k in (1, 2, 3)]
    crossing += [(-k, level < k, waits_down, cube == 0) for k in (1, 2, 3)]

    def across(k):
        return ring_peer((k + RING) % RING)[1]

    barrier = pltpu.get_barrier_semaphore()
    for k, crosses, mine, theirs in crossing:

        @pl.when(jnp.logical_and(crosses, theirs))
        def _():
            pl.semaphore_signal(barrier, inc=1, device_id=across(k), device_id_type=MESH)

    for k in (2, 1, 3):
        for axis in "zxy":
            pl.semaphore_signal(barrier, inc=1, device_id=peer(axis, k)[1], device_id_type=MESH)
    pl.semaphore_signal(barrier, inc=1, device_id=other, device_id_type=MESH)
    entry = 10 + jnp.where(waits_down, 3 - level, 0) + jnp.where(waits_up, level, 0)
    greetings = jnp.where(waits_down, 0, 3 - level) + jnp.where(waits_up, 0, level)

    loads = []
    for g in range(GROUPS):
        columns = pl.ds(g * GROUP, GROUP)
        loads.append(
            pltpu.make_async_copy(g_hbm.at[0, 0, :, columns], g_ref.at[:, columns], load_sems.at[g])
        )
    b_load = pltpu.make_async_copy(b_hbm, b_ref, load_sems.at[GROUPS + 1])
    m_load = pltpu.make_async_copy(m_hbm.at[0], m_ref, load_sems.at[GROUPS])
    b_load.start()
    for load in loads:
        load.start()
    m_load.start()

    turned = {order: permutation(order) for order in ("xyz", "yxz", "zxy")}
    stack[...] = jnp.zeros_like(stack)
    band_stack[...] = jnp.zeros_like(band_stack)

    def remote(source, target, sends, recvs, index, device):
        return pltpu.make_async_remote_copy(
            src_ref=source,
            dst_ref=target,
            send_sem=sends.at[index],
            recv_sem=recvs.at[index],
            device_id=device,
            device_id_type=MESH,
        )

    def rows(place, count):
        return pl.ds(pl.multiple_of(place * count, count), count)

    def copies(c, phase):
        order, first, width = CHUNKS[c]
        t_ref, s_ref, u_ref, r1, r2, r3, ra, rb = per[8 * c : 8 * c + 8]
        result = []
        for k in (2, 1, 3):
            there, device = peer(order[phase], k)
            if phase == 0:
                source, target = t_ref.at[rows(there, 32)], r1.at[k - 1]
            elif phase == 1:
                source, target = s_ref.at[rows(there, 8)], r2.at[k - 1]
            else:
                source, target = u_ref.at[there], r3.at[k - 1]
            index = c * 12 + (phase * 3 + 3 if phase else 0) + k - 1
            result.append(remote(source, target, send_sems, recv_sems, index, device))
        return result

    def hops(c, step, begin=0, end=4):
        order, first, width = CHUNKS[c]
        t_ref, s_ref, u_ref, r1, r2, r3, ra, rb = per[8 * c : 8 * c + 8]
        cut = half(width)
        one, two = pl.ds(0, cut), pl.ds(cut, width - cut)
        far = peer(order[0], 2)[0]
        after, up = peer(order[0], 1)
        before, down = peer(order[0], 3)
        if step == 0:
            moves = [
                (t_ref.at[rows(far, 32), one], ra, up),
                (t_ref.at[rows(far, 32), two], rb, down),
                (t_ref.at[rows(after, 32), two], r1.at[0, :, two], up),
                (t_ref.at[rows(before, 32), one], r1.at[1, :, one], down),
            ]
        else:
            moves = [
                (t_ref.at[rows(after, 32), one], r1.at[0, :, one], up),
                (t_ref.at[rows(before, 32), two], r1.at[1, :, two], down),
            ]
        return [
            remote(source, target, send_sems, recv_sems, c * 12 + step * 4 + j, device)
            for j, (source, target, device) in enumerate(moves)
            if begin <= j < end
        ]

    def low_copies(n, phase):
        order = SETS[n][0]
        l_ref, k_ref, v_ref, s_ref, r1, r2 = low_per[6 * n : 6 * n + 6]
        result = []
        for k in (2, 1, 3):
            there, device = peer(order[phase], k)
            if phase == 0:
                source, target = v_ref.at[rows(there, 16)], r1.at[k - 1]
            else:
                source, target = s_ref.at[there], r2.at[k - 1]
            index = (n * 2 + phase) * 3 + k - 1
            result.append(remote(source, target, low_send, low_recv, index, device))
        return result

    def swap_copy(n):
        l_ref, k_ref = low_per[6 * n : 6 * n + 2]
        return remote(l_ref.at[rows(1 - core, 64)], k_ref, pair_send, pair_recv, n + 1, other)

    def ring_copies():
        result = []
        for k in (8, 7, 9, 6, 10, 5, 11, 4, 12, 3, 13, 2, 14, 1, 15):
            low, device = ring_peer(k)
            result.append(
                remote(ring_out.at[low], ring_in.at[k - 1], ring_send, ring_recv, k - 1, device)
            )
        return result

    def old_copy():
        return remote(old_ref.at[1 - core], old_in, pair_send, pair_recv, len(SETS) + 1, other)

    def pair_copy():
        return remote(pair_out, pair_in, pair_send, pair_recv, 0, other)

    def start(batch):
        for copy in batch:
            copy.start()

    def arrive(batch):
        for copy in batch:
            copy.wait_recv()

    def turn(c):
        order, first, width = CHUNKS[c]
        per[8 * c][...] = jnp.dot(
            turned[order], g_ref[:, first : first + width], preferred_element_type=jnp.float32
        )

    def low_first(n):
        order, first, count = SETS[n]
        place = band_permutation(order)
        parts = []
        for j in range(count):
            begin = (first + j) * GROUP
            both = jnp.dot(
                g_ref[:, begin : begin + GROUP], b_ref[...], preferred_element_type=jnp.float32
            )
            parts.append(both[:, :128] + both[:, 128:])
        high, low = split(jnp.concatenate(parts, axis=1))
        low_per[6 * n][...] = jnp.dot(place, high, preferred_element_type=jnp.float32) + jnp.dot(
            place, low, preferred_element_type=jnp.float32
        )
        swap_copy(n).start()

    def low_swapped(n):
        l_ref, k_ref, v_ref, s_ref, r1, r2 = low_per[6 * n : 6 * n + 6]
        arrive([swap_copy(n)])
        v_ref[...] = l_ref[rows(core, 64), :] + k_ref[...]
        start(low_copies(n, 0))

    def low_second(n):
        l_ref, k_ref, v_ref, s_ref, r1, r2 = low_per[6 * n : 6 * n + 6]
        arrive(low_copies(n, 0))
        total = (v_ref[rows(at[SETS[n][0][0]], 16), :] + r1[0]) + (r1[1] + r1[2])
        for q in range(4):
            s_ref[q] = total[4 * q : 4 * q + 4]
        start(low_copies(n, 1))

    def low_third(n):
        l_ref, k_ref, v_ref, s_ref, r1, r2 = low_per[6 * n : 6 * n + 6]
        order, first, count = SETS[n]
        arrive(low_copies(n, 1))
        total = (s_ref[at[order[1]]] + r2[0]) + (r2[1] + r2[2])
        for q in range(4):
            ring_out[q, :, first * 128 : (first + count) * 128] = total[q : q + 1]

    def relayed(c):
        order, first, width = CHUNKS[c]
        t_ref, s_ref, u_ref, r1, r2, r3, ra, rb = per[8 * c : 8 * c + 8]
        cut = half(width)
        arrive(hops(c, 0, 0, 2))
        after, before = rows(peer(order[0], 1)[0], 32), rows(peer(order[0], 3)[0], 32)
        t_ref[after, :cut] = t_ref[after, :cut] + ra[...]
        t_ref[before, cut:] = t_ref[before, cut:] + rb[...]
        start(hops(c, 1))

    def second(c):
        order, first, width = CHUNKS[c]
        t_ref, s_ref, u_ref, r1, r2, r3, ra, rb = per[8 * c : 8 * c + 8]
        own = rows(at[order[0]], 32)
        if order[0] == "z":
            arrive(copies(c, 0))
            s_ref[...] = (t_ref[own, :] + r1[0]) + (r1[1] + r1[2])
        else:
            arrive(hops(c, 0, 2) + hops(c, 1))
            s_ref[...] = t_ref[own, :] + (r1[0] + r1[1])
        start(copies(c, 1))

    def third(c):
        order, first, width = CHUNKS[c]
        t_ref, s_ref, u_ref, r1, r2, r3, ra, rb = per[8 * c : 8 * c + 8]
        arrive(copies(c, 1))
        own = pl.ds(pl.multiple_of(at[order[1]] * 8, 8), 8)
        total = (s_ref[own, :] + r2[0]) + (r2[1] + r2[2])
        for q in range(4):
            u_ref[q] = total[2 * q : 2 * q + 2]
        start(copies(c, 2))

    def last(c):
        order, first, width = CHUNKS[c]
        t_ref, s_ref, u_ref, r1, r2, r3, ra, rb = per[8 * c : 8 * c + 8]
        arrive(copies(c, 2))
        total = (u_ref[at[order[2]]] + r3[0]) + (r3[1] + r3[2])
        blended = DECAY * m_ref[:, first : first + width] + total
        begin = first
        while begin < first + width:
            g = begin // GROUP
            end = min(first + width, (g + 1) * GROUP)
            stack[2 * g : 2 * g + 2, begin - g * GROUP : end - g * GROUP] = blended[
                :, begin - first : end - first
            ]
            begin = end

    def low_fourth():
        arrive(ring_copies())
        terms = [ring_out[at["z"]]] + [ring_in[k] for k in range(RING - 1)]
        while len(terms) > 1:
            terms = [terms[j] + terms[j + 1] for j in range(0, len(terms), 2)]
        pair_out[...] = terms[0]
        pair_copy().start()

    def relay_signal(j):
        for k in (3, 13):
            pl.semaphore_signal(
                relay.at[j], inc=1, device_id=ring_peer(k)[1], device_id_type=MESH
            )

    def greet():
        for k, crosses, mine, theirs in crossing:

            @pl.when(jnp.logical_and(crosses, mine))
            def _():
                pl.semaphore_signal(relay.at[2], inc=1, device_id=across(k), device_id_type=MESH)

    def stage(number, when):
        @pl.when(when)
        def _():
            if number == 0:
                @pl.when(greetings > 0)
                def _():
                    pl.semaphore_wait(relay.at[2], greetings)

                relay_signal(0)
            elif number == 1:
                pl.semaphore_wait(relay.at[0], 2)
                relay_signal(1)
            else:
                pl.semaphore_wait(relay.at[1], 2)
                start(ring_copies())

    early, late = cube > 0, cube == 0
    loads[0].wait()
    turn(0)
    pl.semaphore_wait(barrier, entry)
    greet()
    start(hops(0, 0))
    loads[1].wait()
    turn(1)
    start(hops(1, 0))
    loads[2].wait()
    turn(2)
    start(copies(2, 0))
    b_load.wait()
    low_first(0)
    loads[3].wait()
    loads[4].wait()
    low_first(1)
    low_swapped(0)
    low_swapped(1)
    stage(0, early)
    for c in range(3, N_CHUNKS):
        turn(c)
    m_load.wait()
    high, low = b_ref[:, :128], b_ref[:, 128:]
    old = DECAY * m_ref[...]
    for g in range(GROUPS):
        stack[2 * g : 2 * g + 2, :] = old[:, g * GROUP : (g + 1) * GROUP]
    old_band = analyse(stack[...], high, low)
    for g in range(GROUPS):
        for i in range(2):
            old_ref[i, :, g * 128 : (g + 1) * 128] = old_band[2 * g + i : 2 * g + i + 1]
    start([old_copy()])
    relayed(0)
    relayed(1)
    start(hops(3, 0))
    start(hops(4, 0))
    for n in range(len(SETS)):
        low_second(n)
    stage(1, early)
    start(hops(5, 0))
    start(hops(6, 0))
    relayed(3)
    relayed(4)
    stage(0, late)
    for n in range(len(SETS)):
        low_third(n)
    arrive([old_copy()])
    ring_out[at["z"]] = ring_out[at["z"]] + (old_ref[core] + old_in[...])
    stage(2, early)
    second(0)
    second(1)
    second(2)
    stage(1, late)
    relayed(5)
    relayed(6)
    third(0)
    third(1)
    second(3)
    second(4)
    stage(2, late)
    third(2)
    second(5)
    second(6)
    last(0)
    last(1)
    third(3)
    third(4)
    last(2)
    third(5)
    third(6)
    low_fourth()
    last(3)
    last(4)
    last(5)
    last(6)
    blended = stack[...]
    fresh = blended - expand(analyse(blended, high, low), high, low)
    for g in range(GROUPS):
        fresh_ref[0, :, g * GROUP : (g + 1) * GROUP] = fresh[2 * g : 2 * g + 2]
    arrive([pair_copy()])
    for g in range(GROUPS):
        lanes = slice(g * 128, (g + 1) * 128)
        mine, theirs = pair_out[:, lanes], pair_in[:, lanes]
        band_stack[2 * g : 2 * g + 1, :] = jnp.where(core == 0, mine, theirs)
        band_stack[2 * g + 1 : 2 * g + 2, :] = jnp.where(core == 0, theirs, mine)
    update = expand(band_stack[...] * (1.0 / REPS), high, low)
    for g in range(GROUPS):
        update_ref[:, g * GROUP : (g + 1) * GROUP] = update[2 * g : 2 * g + 2]
    sent = []
    for c in range(N_CHUNKS):
        sent += copies(c, 0) if CHUNKS[c][0][0] == "z" else hops(c, 0) + hops(c, 1)
        sent += copies(c, 1) + copies(c, 2)
    sent += [copy for n in range(len(SETS)) for phase in range(2) for copy in low_copies(n, phase)]
    sent += ring_copies() + [pair_copy(), old_copy()] + [swap_copy(n) for n in range(len(SETS))]
    for copy in sent:
        copy.wait_send()


def shards(gradients, momentum):
    basis = jnp.asarray(halves())
    f32 = jnp.float32
    per = []
    for order, first, width in CHUNKS:
        per += [
            pltpu.VMEM((ROWS, width), f32),
            pltpu.VMEM((32, width), f32),
            pltpu.VMEM((4, 2, width), f32),
            pltpu.VMEM((3 if order[0] == "z" else 2, 32, width), f32),
            pltpu.VMEM((3, 8, width), f32),
            pltpu.VMEM((3, 2, width), f32),
            pltpu.VMEM((32, half(width)), f32),
            pltpu.VMEM((32, width - half(width)), f32),
        ]
    low_per = []
    for order, first, count in SETS:
        width = count * 128
        low_per += [
            pltpu.VMEM((ROWS, width), f32),
            pltpu.VMEM((64, width), f32),
            pltpu.VMEM((64, width), f32),
            pltpu.VMEM((4, 4, width), f32),
            pltpu.VMEM((3, 16, width), f32),
            pltpu.VMEM((3, 4, width), f32),
        ]
    return pl.pallas_call(
        kernel,
        out_shape=(
            jax.ShapeDtypeStruct((1, 2, D), f32),
            jax.ShapeDtypeStruct((2, D), f32),
        ),
        in_specs=[pl.BlockSpec(memory_space=pltpu.HBM)] * 3,
        out_specs=(pl.BlockSpec(memory_space=pltpu.VMEM),) * 2,
        scratch_shapes=[
            pltpu.VMEM((ROWS, D), jnp.bfloat16),
            pltpu.VMEM((2, D), f32),
            pltpu.VMEM((GROUP, 256), jnp.bfloat16),
            pltpu.VMEM((16, GROUP), f32),
            pltpu.VMEM((16, 128), f32),
            *per,
            *low_per,
            pltpu.VMEM((4, 1, BANDS), f32),
            pltpu.VMEM((RING - 1, 1, BANDS), f32),
            pltpu.VMEM((1, BANDS), f32),
            pltpu.VMEM((1, BANDS), f32),
            pltpu.VMEM((2, 1, BANDS), f32),
            pltpu.VMEM((1, BANDS), f32),
            pltpu.SemaphoreType.DMA((GROUPS + 2,)),
            pltpu.SemaphoreType.DMA((12 * N_CHUNKS,)),
            pltpu.SemaphoreType.DMA((12 * N_CHUNKS,)),
            pltpu.SemaphoreType.DMA((6 * len(SETS),)),
            pltpu.SemaphoreType.DMA((6 * len(SETS),)),
            pltpu.SemaphoreType.DMA((RING - 1,)),
            pltpu.SemaphoreType.DMA((RING - 1,)),
            pltpu.SemaphoreType.DMA((len(SETS) + 2,)),
            pltpu.SemaphoreType.DMA((len(SETS) + 2,)),
            pltpu.SemaphoreType.REGULAR((3,)),
        ],
        compiler_params=pltpu.CompilerParams(
            collective_id=0, has_side_effects=True, vmem_limit_bytes=55136 << 10
        ),
        name="momentum_step",
    )(gradients, momentum, basis)


def solution(mesh):
    return jax.shard_map(
        shards,
        mesh=mesh,
        in_specs=(P("rep", "fsdp", None, None), P("rep", "fsdp", None)),
        out_specs=(P("rep", "fsdp", None), P("fsdp", None)),
        check_vma=False,
    )
```

```python
import jax
import jax.numpy as jnp
import ml_dtypes
import numpy as np
from jax import lax
from jax.experimental import pallas as pl
from jax.experimental.pallas import tpu as pltpu
from jax.sharding import PartitionSpec as P

SPAN = 64
BAND = 8
D = 5120
ROWS = 128
GROUP = 1024
GROUPS = D // GROUP
DECAY = 0.9
MESH = pl.DeviceIdType.MESH

REPS = 8
RING = 16

CHUNKS = (
    ("xyz", 0, 896),
    ("yxz", 896, 896),
    ("zxy", 1792, 768),
    ("xyz", 2560, 896),
    ("yxz", 3456, 896),
    ("xyz", 4352, 384),
    ("yxz", 4736, 384),
)
N_CHUNKS = len(CHUNKS)
SETS = (("xyz", 0, 2), ("yxz", 2, 3))
BANDS = D // SPAN * BAND


def halves():
    freq = np.arange(BAND)[:, None]
    place = np.arange(SPAN)[None, :]
    table = np.cos(np.pi * (2.0 * place + 1.0) * freq / (2.0 * SPAN)) * np.sqrt(2.0 / SPAN)
    table = table * np.where(freq == 0, np.sqrt(0.5), 1.0)
    full = np.zeros((GROUP, GROUP // SPAN * BAND), np.float32)
    for block in range(GROUP // SPAN):
        full[block * SPAN : (block + 1) * SPAN, block * BAND : (block + 1) * BAND] = table.T
    high = full.astype(ml_dtypes.bfloat16)
    low = (full - high.astype(np.float32)).astype(ml_dtypes.bfloat16)
    return np.concatenate([high, low], axis=1)


def half(width):
    return (width // 128 + 1) // 2 * 128


def selector(source):
    column = lax.broadcasted_iota(jnp.int32, (ROWS, ROWS), 1)
    return jnp.where(source == column, 1.0, 0.0).astype(jnp.bfloat16)


WEIGHT = {"y": 32, "z": 8, "x": 2}


def permutation(order):
    row = lax.broadcasted_iota(jnp.int32, (ROWS, ROWS), 0)
    return selector(
        ((row >> 5) & 3) * WEIGHT[order[0]]
        + ((row >> 3) & 3) * WEIGHT[order[1]]
        + ((row >> 1) & 3) * WEIGHT[order[2]]
        + (row & 1)
    )


def band_permutation(order):
    row = lax.broadcasted_iota(jnp.int32, (ROWS, ROWS), 0)
    return selector(
        ((row >> 4) & 3) * WEIGHT[order[0]]
        + ((row >> 2) & 3) * WEIGHT[order[1]]
        + (row & 3) * WEIGHT[order[2]]
        + (row >> 6)
    )


def split(value):
    high = value.astype(jnp.bfloat16)
    return high, (value - high.astype(jnp.float32)).astype(jnp.bfloat16)


def analyse(value, basis_high, basis_low):
    high, low = split(value)
    dims = (((1,), (0,)), ((), ()))
    f32 = jnp.float32
    return (
        lax.dot_general(high, basis_high, dims, preferred_element_type=f32)
        + lax.dot_general(high, basis_low, dims, preferred_element_type=f32)
        + lax.dot_general(low, basis_high, dims, preferred_element_type=f32)
    )


def expand(value, basis_high, basis_low):
    high, low = split(value)
    dims = (((1,), (1,)), ((), ()))
    f32 = jnp.float32
    return (
        lax.dot_general(high, basis_high, dims, preferred_element_type=f32)
        + lax.dot_general(high, basis_low, dims, preferred_element_type=f32)
        + lax.dot_general(low, basis_high, dims, preferred_element_type=f32)
    )


def kernel(g_hbm, m_hbm, b_hbm, fresh_ref, update_ref, *scratch):
    scratch = list(scratch)
    take = lambda n: [scratch.pop(0) for _ in range(n)]
    g_ref, m_ref, b_ref, stack, band_stack = take(5)
    per = take(8 * N_CHUNKS)
    low_per = take(6 * len(SETS))
    ring_out, ring_in, pair_out, pair_in, old_ref, old_in = take(6)
    load_sems, send_sems, recv_sems, low_send, low_recv = take(5)
    ring_send, ring_recv, pair_send, pair_recv, relay = take(5)

    rep = lax.axis_index("rep")
    fsdp = lax.axis_index("fsdp")
    core = rep % 2
    at = {"y": fsdp // 16, "z": (fsdp // 4) % 4, "x": fsdp % 4}
    stride = {"y": 16, "z": 4, "x": 1}
    height = (rep // 2) * 4 + at["z"]

    def peer(axis, k):
        there = lax.rem(at[axis] + k, 4)
        return there, {"rep": rep, "fsdp": fsdp + (there - at[axis]) * stride[axis]}

    def ring_peer(k):
        there = lax.rem(height + k, RING)
        low = there % 4
        return low, {"rep": (there // 4) * 2 + core, "fsdp": fsdp + (low - at["z"]) * 4}

    other = {"rep": rep + 1 - 2 * core, "fsdp": fsdp}

    cube, level = rep // 2, at["z"]
    waits_down, waits_up = cube >= 1, cube == 3
    crossing = [(k, level + k > 3, waits_up, cube < 3) for k in (1, 2, 3)]
    crossing += [(-k, level < k, waits_down, cube == 0) for k in (1, 2, 3)]

    def across(k):
        return ring_peer((k + RING) % RING)[1]

    barrier = pltpu.get_barrier_semaphore()
    for k, crosses, mine, theirs in crossing:

        @pl.when(jnp.logical_and(crosses, theirs))
        def _():
            pl.semaphore_signal(barrier, inc=1, device_id=across(k), device_id_type=MESH)

    for k in (2, 1, 3):
        for axis in "zxy":
            pl.semaphore_signal(barrier, inc=1, device_id=peer(axis, k)[1], device_id_type=MESH)
    pl.semaphore_signal(barrier, inc=1, device_id=other, device_id_type=MESH)
    entry = 10 + jnp.where(waits_down, 3 - level, 0) + jnp.where(waits_up, level, 0)
    greetings = jnp.where(waits_down, 0, 3 - level) + jnp.where(waits_up, 0, level)

    loads = []
    for g in range(GROUPS):
        columns = pl.ds(g * GROUP, GROUP)
        loads.append(
            pltpu.make_async_copy(g_hbm.at[0, 0, :, columns], g_ref.at[:, columns], load_sems.at[g])
        )
    b_load = pltpu.make_async_copy(b_hbm, b_ref, load_sems.at[GROUPS + 1])
    m_load = pltpu.make_async_copy(m_hbm.at[0], m_ref, load_sems.at[GROUPS])
    b_load.start()
    for load in loads:
        load.start()
    m_load.start()

    turned = {order: permutation(order) for order in ("xyz", "yxz", "zxy")}
    stack[...] = jnp.zeros_like(stack)
    band_stack[...] = jnp.zeros_like(band_stack)

    def remote(source, target, sends, recvs, index, device):
        return pltpu.make_async_remote_copy(
            src_ref=source,
            dst_ref=target,
            send_sem=sends.at[index],
            recv_sem=recvs.at[index],
            device_id=device,
            device_id_type=MESH,
        )

    def rows(place, count):
        return pl.ds(pl.multiple_of(place * count, count), count)

    def copies(c, phase):
        order, first, width = CHUNKS[c]
        t_ref, s_ref, u_ref, r1, r2, r3, ra, rb = per[8 * c : 8 * c + 8]
        result = []
        for k in (2, 1, 3):
            there, device = peer(order[phase], k)
            if phase == 0:
                source, target = t_ref.at[rows(there, 32)], r1.at[k - 1]
            elif phase == 1:
                source, target = s_ref.at[rows(there, 8)], r2.at[k - 1]
            else:
                source, target = u_ref.at[there], r3.at[k - 1]
            index = c * 12 + (phase * 3 + 3 if phase else 0) + k - 1
            result.append(remote(source, target, send_sems, recv_sems, index, device))
        return result

    def hops(c, step, begin=0, end=4):
        order, first, width = CHUNKS[c]
        t_ref, s_ref, u_ref, r1, r2, r3, ra, rb = per[8 * c : 8 * c + 8]
        cut = half(width)
        one, two = pl.ds(0, cut), pl.ds(cut, width - cut)
        far = peer(order[0], 2)[0]
        after, up = peer(order[0], 1)
        before, down = peer(order[0], 3)
        if step == 0:
            moves = [
                (t_ref.at[rows(far, 32), one], ra, up),
                (t_ref.at[rows(far, 32), two], rb, down),
                (t_ref.at[rows(after, 32), two], r1.at[0, :, two], up),
                (t_ref.at[rows(before, 32), one], r1.at[1, :, one], down),
            ]
        else:
            moves = [
                (t_ref.at[rows(after, 32), one], r1.at[0, :, one], up),
                (t_ref.at[rows(before, 32), two], r1.at[1, :, two], down),
            ]
        return [
            remote(source, target, send_sems, recv_sems, c * 12 + step * 4 + j, device)
            for j, (source, target, device) in enumerate(moves)
            if begin <= j < end
        ]

    def low_copies(n, phase):
        order = SETS[n][0]
        l_ref, k_ref, v_ref, s_ref, r1, r2 = low_per[6 * n : 6 * n + 6]
        result = []
        for k in (2, 1, 3):
            there, device = peer(order[phase], k)
            if phase == 0:
                source, target = v_ref.at[rows(there, 16)], r1.at[k - 1]
            else:
                source, target = s_ref.at[there], r2.at[k - 1]
            index = (n * 2 + phase) * 3 + k - 1
            result.append(remote(source, target, low_send, low_recv, index, device))
        return result

    def swap_copy(n):
        l_ref, k_ref = low_per[6 * n : 6 * n + 2]
        return remote(l_ref.at[rows(1 - core, 64)], k_ref, pair_send, pair_recv, n + 1, other)

    def ring_copies():
        result = []
        for k in (8, 7, 9, 6, 10, 5, 11, 4, 12, 3, 13, 2, 14, 1, 15):
            low, device = ring_peer(k)
            result.append(
                remote(ring_out.at[low], ring_in.at[k - 1], ring_send, ring_recv, k - 1, device)
            )
        return result

    def old_copy():
        return remote(old_ref.at[1 - core], old_in, pair_send, pair_recv, len(SETS) + 1, other)

    def pair_copy():
        return remote(pair_out, pair_in, pair_send, pair_recv, 0, other)

    def start(batch):
        for copy in batch:
            copy.start()

    def arrive(batch):
        for copy in batch:
            copy.wait_recv()

    def turn(c):
        order, first, width = CHUNKS[c]
        per[8 * c][...] = jnp.dot(
            turned[order], g_ref[:, first : first + width], preferred_element_type=jnp.float32
        )

    def low_first(n):
        order, first, count = SETS[n]
        place = band_permutation(order)
        parts = []
        for j in range(count):
            begin = (first + j) * GROUP
            both = jnp.dot(
                g_ref[:, begin : begin + GROUP], b_ref[...], preferred_element_type=jnp.float32
            )
            parts.append(both[:, :128] + both[:, 128:])
        high, low = split(jnp.concatenate(parts, axis=1))
        low_per[6 * n][...] = jnp.dot(place, high, preferred_element_type=jnp.float32) + jnp.dot(
            place, low, preferred_element_type=jnp.float32
        )
        swap_copy(n).start()

    def low_swapped(n):
        l_ref, k_ref, v_ref, s_ref, r1, r2 = low_per[6 * n : 6 * n + 6]
        arrive([swap_copy(n)])
        v_ref[...] = l_ref[rows(core, 64), :] + k_ref[...]
        start(low_copies(n, 0))

    def low_second(n):
        l_ref, k_ref, v_ref, s_ref, r1, r2 = low_per[6 * n : 6 * n + 6]
        arrive(low_copies(n, 0))
        total = (v_ref[rows(at[SETS[n][0][0]], 16), :] + r1[0]) + (r1[1] + r1[2])
        for q in range(4):
            s_ref[q] = total[4 * q : 4 * q + 4]
        start(low_copies(n, 1))

    def low_third(n):
        l_ref, k_ref, v_ref, s_ref, r1, r2 = low_per[6 * n : 6 * n + 6]
        order, first, count = SETS[n]
        arrive(low_copies(n, 1))
        total = (s_ref[at[order[1]]] + r2[0]) + (r2[1] + r2[2])
        for q in range(4):
            ring_out[q, :, first * 128 : (first + count) * 128] = total[q : q + 1]

    def relayed(c):
        order, first, width = CHUNKS[c]
        t_ref, s_ref, u_ref, r1, r2, r3, ra, rb = per[8 * c : 8 * c + 8]
        cut = half(width)
        arrive(hops(c, 0, 0, 2))
        after, before = rows(peer(order[0], 1)[0], 32), rows(peer(order[0], 3)[0], 32)
        t_ref[after, :cut] = t_ref[after, :cut] + ra[...]
        t_ref[before, cut:] = t_ref[before, cut:] + rb[...]
        start(hops(c, 1))

    def second(c):
        order, first, width = CHUNKS[c]
        t_ref, s_ref, u_ref, r1, r2, r3, ra, rb = per[8 * c : 8 * c + 8]
        own = rows(at[order[0]], 32)
        if order[0] == "z":
            arrive(copies(c, 0))
            s_ref[...] = (t_ref[own, :] + r1[0]) + (r1[1] + r1[2])
        else:
            arrive(hops(c, 0, 2) + hops(c, 1))
            s_ref[...] = t_ref[own, :] + (r1[0] + r1[1])
        start(copies(c, 1))

    def third(c):
        order, first, width = CHUNKS[c]
        t_ref, s_ref, u_ref, r1, r2, r3, ra, rb = per[8 * c : 8 * c + 8]
        arrive(copies(c, 1))
        own = pl.ds(pl.multiple_of(at[order[1]] * 8, 8), 8)
        total = (s_ref[own, :] + r2[0]) + (r2[1] + r2[2])
        for q in range(4):
            u_ref[q] = total[2 * q : 2 * q + 2]
        start(copies(c, 2))

    def last(c):
        order, first, width = CHUNKS[c]
        t_ref, s_ref, u_ref, r1, r2, r3, ra, rb = per[8 * c : 8 * c + 8]
        arrive(copies(c, 2))
        total = (u_ref[at[order[2]]] + r3[0]) + (r3[1] + r3[2])
        blended = DECAY * m_ref[:, first : first + width] + total
        begin = first
        while begin < first + width:
            g = begin // GROUP
            end = min(first + width, (g + 1) * GROUP)
            stack[2 * g : 2 * g + 2, begin - g * GROUP : end - g * GROUP] = blended[
                :, begin - first : end - first
            ]
            begin = end

    def low_fourth():
        arrive(ring_copies())
        terms = [ring_out[at["z"]]] + [ring_in[k] for k in range(RING - 1)]
        while len(terms) > 1:
            terms = [terms[j] + terms[j + 1] for j in range(0, len(terms), 2)]
        pair_out[...] = terms[0]
        pair_copy().start()

    def relay_signal(j):
        for k in (3, 13):
            pl.semaphore_signal(
                relay.at[j], inc=1, device_id=ring_peer(k)[1], device_id_type=MESH
            )

    def greet():
        for k, crosses, mine, theirs in crossing:

            @pl.when(jnp.logical_and(crosses, mine))
            def _():
                pl.semaphore_signal(relay.at[2], inc=1, device_id=across(k), device_id_type=MESH)

    def stage(number, when):
        @pl.when(when)
        def _():
            if number == 0:
                @pl.when(greetings > 0)
                def _():
                    pl.semaphore_wait(relay.at[2], greetings)

                relay_signal(0)
            elif number == 1:
                pl.semaphore_wait(relay.at[0], 2)
                relay_signal(1)
            else:
                pl.semaphore_wait(relay.at[1], 2)
                start(ring_copies())

    early, late = cube > 0, cube == 0
    loads[0].wait()
    turn(0)
    pl.semaphore_wait(barrier, entry)
    greet()
    start(hops(0, 0))
    loads[1].wait()
    turn(1)
    start(hops(1, 0))
    loads[2].wait()
    turn(2)
    start(copies(2, 0))
    b_load.wait()
    low_first(0)
    loads[3].wait()
    loads[4].wait()
    low_first(1)
    low_swapped(0)
    low_swapped(1)
    stage(0, early)
    for c in range(3, N_CHUNKS):
        turn(c)
    m_load.wait()
    high, low = b_ref[:, :128], b_ref[:, 128:]
    old = DECAY * m_ref[...]
    for g in range(GROUPS):
        stack[2 * g : 2 * g + 2, :] = old[:, g * GROUP : (g + 1) * GROUP]
    old_band = analyse(stack[...], high, low)
    for g in range(GROUPS):
        for i in range(2):
            old_ref[i, :, g * 128 : (g + 1) * 128] = old_band[2 * g + i : 2 * g + i + 1]
    start([old_copy()])
    relayed(0)
    relayed(1)
    start(hops(3, 0))
    start(hops(4, 0))
    for n in range(len(SETS)):
        low_second(n)
    stage(1, early)
    start(hops(5, 0))
    start(hops(6, 0))
    relayed(3)
    relayed(4)
    stage(0, late)
    for n in range(len(SETS)):
        low_third(n)
    arrive([old_copy()])
    ring_out[at["z"]] = ring_out[at["z"]] + (old_ref[core] + old_in[...])
    stage(2, early)
    second(0)
    second(1)
    second(2)
    stage(1, late)
    relayed(5)
    relayed(6)
    third(0)
    third(1)
    second(3)
    second(4)
    stage(2, late)
    third(2)
    second(5)
    second(6)
    last(0)
    last(1)
    third(3)
    third(4)
    last(2)
    third(5)
    third(6)
    low_fourth()
    last(3)
    last(4)
    last(5)
    last(6)
    blended = stack[...]
    fresh = blended - expand(analyse(blended, high, low), high, low)
    for g in range(GROUPS):
        fresh_ref[0, :, g * GROUP : (g + 1) * GROUP] = fresh[2 * g : 2 * g + 2]
    arrive([pair_copy()])
    for g in range(GROUPS):
        lanes = slice(g * 128, (g + 1) * 128)
        mine, theirs = pair_out[:, lanes], pair_in[:, lanes]
        band_stack[2 * g : 2 * g + 1, :] = jnp.where(core == 0, mine, theirs)
        band_stack[2 * g + 1 : 2 * g + 2, :] = jnp.where(core == 0, theirs, mine)
    update = expand(band_stack[...] * (1.0 / REPS), high, low)
    for g in range(GROUPS):
        update_ref[:, g * GROUP : (g + 1) * GROUP] = update[2 * g : 2 * g + 2]
    sent = []
    for c in range(N_CHUNKS):
        sent += copies(c, 0) if CHUNKS[c][0][0] == "z" else hops(c, 0) + hops(c, 1)
        sent += copies(c, 1) + copies(c, 2)
    sent += [copy for n in range(len(SETS)) for phase in range(2) for copy in low_copies(n, phase)]
    sent += ring_copies() + [pair_copy(), old_copy()] + [swap_copy(n) for n in range(len(SETS))]
    for copy in sent:
        copy.wait_send()


def shards(gradients, momentum):
    basis = jnp.asarray(halves())
    f32 = jnp.float32
    per = []
    for order, first, width in CHUNKS:
        per += [
            pltpu.VMEM((ROWS, width), f32),
            pltpu.VMEM((32, width), f32),
            pltpu.VMEM((4, 2, width), f32),
            pltpu.VMEM((3 if order[0] == "z" else 2, 32, width), f32),
            pltpu.VMEM((3, 8, width), f32),
            pltpu.VMEM((3, 2, width), f32),
            pltpu.VMEM((32, half(width)), f32),
            pltpu.VMEM((32, width - half(width)), f32),
        ]
    low_per = []
    for order, first, count in SETS:
        width = count * 128
        low_per += [
            pltpu.VMEM((ROWS, width), f32),
            pltpu.VMEM((64, width), f32),
            pltpu.VMEM((64, width), f32),
            pltpu.VMEM((4, 4, width), f32),
            pltpu.VMEM((3, 16, width), f32),
            pltpu.VMEM((3, 4, width), f32),
        ]
    return pl.pallas_call(
        kernel,
        out_shape=(
            jax.ShapeDtypeStruct((1, 2, D), f32),
            jax.ShapeDtypeStruct((2, D), f32),
        ),
        in_specs=[pl.BlockSpec(memory_space=pltpu.HBM)] * 3,
        out_specs=(pl.BlockSpec(memory_space=pltpu.VMEM),) * 2,
        scratch_shapes=[
            pltpu.VMEM((ROWS, D), jnp.bfloat16),
            pltpu.VMEM((2, D), f32),
            pltpu.VMEM((GROUP, 256), jnp.bfloat16),
            pltpu.VMEM((16, GROUP), f32),
            pltpu.VMEM((16, 128), f32),
            *per,
            *low_per,
            pltpu.VMEM((4, 1, BANDS), f32),
            pltpu.VMEM((RING - 1, 1, BANDS), f32),
            pltpu.VMEM((1, BANDS), f32),
            pltpu.VMEM((1, BANDS), f32),
            pltpu.VMEM((2, 1, BANDS), f32),
            pltpu.VMEM((1, BANDS), f32),
            pltpu.SemaphoreType.DMA((GROUPS + 2,)),
            pltpu.SemaphoreType.DMA((12 * N_CHUNKS,)),
            pltpu.SemaphoreType.DMA((12 * N_CHUNKS,)),
            pltpu.SemaphoreType.DMA((6 * len(SETS),)),
            pltpu.SemaphoreType.DMA((6 * len(SETS),)),
            pltpu.SemaphoreType.DMA((RING - 1,)),
            pltpu.SemaphoreType.DMA((RING - 1,)),
            pltpu.SemaphoreType.DMA((len(SETS) + 2,)),
            pltpu.SemaphoreType.DMA((len(SETS) + 2,)),
            pltpu.SemaphoreType.REGULAR((3,)),
        ],
        compiler_params=pltpu.CompilerParams(
            collective_id=0, has_side_effects=True, vmem_limit_bytes=55136 << 10
        ),
        name="momentum_step",
    )(gradients, momentum, basis)


def solution(mesh):
    return jax.shard_map(
        shards,
        mesh=mesh,
        in_specs=(P("rep", "fsdp", None, None), P("rep", "fsdp", None)),
        out_specs=(P("rep", "fsdp", None), P("fsdp", None)),
        check_vma=False,
    )
```

```python
import jax
import jax.numpy as jnp
import ml_dtypes
import numpy as np
from jax import lax
from jax.experimental import pallas as pl
from jax.experimental.pallas import tpu as pltpu
from jax.sharding import PartitionSpec as P

SPAN = 64
BAND = 8
D = 5120
ROWS = 128
GROUP = 1024
GROUPS = D // GROUP
DECAY = 0.9
MESH = pl.DeviceIdType.MESH

REPS = 8
RING = 16

CHUNKS = (
    ("xyz", 0, 896),
    ("yxz", 896, 896),
    ("zxy", 1792, 1024),
    ("xyz", 2816, 640),
    ("yxz", 3456, 640),
    ("xyz", 4096, 512),
    ("yxz", 4608, 512),
)
N_CHUNKS = len(CHUNKS)
SETS = (("xyz", 0, 2), ("yxz", 2, 3))
BANDS = D // SPAN * BAND


def halves():
    freq = np.arange(BAND)[:, None]
    place = np.arange(SPAN)[None, :]
    table = np.cos(np.pi * (2.0 * place + 1.0) * freq / (2.0 * SPAN)) * np.sqrt(2.0 / SPAN)
    table = table * np.where(freq == 0, np.sqrt(0.5), 1.0)
    full = np.zeros((GROUP, GROUP // SPAN * BAND), np.float32)
    for block in range(GROUP // SPAN):
        full[block * SPAN : (block + 1) * SPAN, block * BAND : (block + 1) * BAND] = table.T
    high = full.astype(ml_dtypes.bfloat16)
    low = (full - high.astype(np.float32)).astype(ml_dtypes.bfloat16)
    return np.concatenate([high, low], axis=1)


def half(width):
    return (width // 128 + 1) // 2 * 128


def selector(source):
    column = lax.broadcasted_iota(jnp.int32, (ROWS, ROWS), 1)
    return jnp.where(source == column, 1.0, 0.0).astype(jnp.bfloat16)


WEIGHT = {"y": 32, "z": 8, "x": 2}


def permutation(order):
    row = lax.broadcasted_iota(jnp.int32, (ROWS, ROWS), 0)
    return selector(
        ((row >> 5) & 3) * WEIGHT[order[0]]
        + ((row >> 3) & 3) * WEIGHT[order[1]]
        + ((row >> 1) & 3) * WEIGHT[order[2]]
        + (row & 1)
    )


def band_permutation(order):
    row = lax.broadcasted_iota(jnp.int32, (ROWS, ROWS), 0)
    return selector(
        ((row >> 4) & 3) * WEIGHT[order[0]]
        + ((row >> 2) & 3) * WEIGHT[order[1]]
        + (row & 3) * WEIGHT[order[2]]
        + (row >> 6)
    )


def split(value):
    high = value.astype(jnp.bfloat16)
    return high, (value - high.astype(jnp.float32)).astype(jnp.bfloat16)


def analyse(value, basis_high, basis_low):
    high, low = split(value)
    dims = (((1,), (0,)), ((), ()))
    f32 = jnp.float32
    return (
        lax.dot_general(high, basis_high, dims, preferred_element_type=f32)
        + lax.dot_general(high, basis_low, dims, preferred_element_type=f32)
        + lax.dot_general(low, basis_high, dims, preferred_element_type=f32)
    )


def expand(value, basis_high, basis_low):
    high, low = split(value)
    dims = (((1,), (1,)), ((), ()))
    f32 = jnp.float32
    return (
        lax.dot_general(high, basis_high, dims, preferred_element_type=f32)
        + lax.dot_general(high, basis_low, dims, preferred_element_type=f32)
        + lax.dot_general(low, basis_high, dims, preferred_element_type=f32)
    )


def kernel(g_hbm, m_hbm, b_hbm, fresh_ref, update_ref, *scratch):
    scratch = list(scratch)
    take = lambda n: [scratch.pop(0) for _ in range(n)]
    g_ref, m_ref, b_ref, stack, band_stack = take(5)
    per = take(8 * N_CHUNKS)
    low_per = take(6 * len(SETS))
    ring_out, ring_in, pair_out, pair_in, old_ref, old_in = take(6)
    load_sems, send_sems, recv_sems, low_send, low_recv = take(5)
    ring_send, ring_recv, pair_send, pair_recv, relay = take(5)

    rep = lax.axis_index("rep")
    fsdp = lax.axis_index("fsdp")
    core = rep % 2
    at = {"y": fsdp // 16, "z": (fsdp // 4) % 4, "x": fsdp % 4}
    stride = {"y": 16, "z": 4, "x": 1}
    height = (rep // 2) * 4 + at["z"]

    def peer(axis, k):
        there = lax.rem(at[axis] + k, 4)
        return there, {"rep": rep, "fsdp": fsdp + (there - at[axis]) * stride[axis]}

    def ring_peer(k):
        there = lax.rem(height + k, RING)
        low = there % 4
        return low, {"rep": (there // 4) * 2 + core, "fsdp": fsdp + (low - at["z"]) * 4}

    other = {"rep": rep + 1 - 2 * core, "fsdp": fsdp}

    cube, level = rep // 2, at["z"]
    waits_down, waits_up = cube >= 1, cube == 3
    crossing = [(k, level + k > 3, waits_up, cube < 3) for k in (1, 2, 3)]
    crossing += [(-k, level < k, waits_down, cube == 0) for k in (1, 2, 3)]

    def across(k):
        return ring_peer((k + RING) % RING)[1]

    barrier = pltpu.get_barrier_semaphore()
    for k, crosses, mine, theirs in crossing:

        @pl.when(jnp.logical_and(crosses, theirs))
        def _():
            pl.semaphore_signal(barrier, inc=1, device_id=across(k), device_id_type=MESH)

    for k in (2, 1, 3):
        for axis in "zxy":
            pl.semaphore_signal(barrier, inc=1, device_id=peer(axis, k)[1], device_id_type=MESH)
    pl.semaphore_signal(barrier, inc=1, device_id=other, device_id_type=MESH)
    entry = 10 + jnp.where(waits_down, 3 - level, 0) + jnp.where(waits_up, level, 0)
    greetings = jnp.where(waits_down, 0, 3 - level) + jnp.where(waits_up, 0, level)

    loads = []
    for g in range(GROUPS):
        columns = pl.ds(g * GROUP, GROUP)
        loads.append(
            pltpu.make_async_copy(g_hbm.at[0, 0, :, columns], g_ref.at[:, columns], load_sems.at[g])
        )
    b_load = pltpu.make_async_copy(b_hbm, b_ref, load_sems.at[GROUPS + 1])
    m_load = pltpu.make_async_copy(m_hbm.at[0], m_ref, load_sems.at[GROUPS])
    b_load.start()
    for load in loads:
        load.start()
    m_load.start()

    turned = {order: permutation(order) for order in ("xyz", "yxz", "zxy")}
    stack[...] = jnp.zeros_like(stack)
    band_stack[...] = jnp.zeros_like(band_stack)

    def remote(source, target, sends, recvs, index, device):
        return pltpu.make_async_remote_copy(
            src_ref=source,
            dst_ref=target,
            send_sem=sends.at[index],
            recv_sem=recvs.at[index],
            device_id=device,
            device_id_type=MESH,
        )

    def rows(place, count):
        return pl.ds(pl.multiple_of(place * count, count), count)

    def copies(c, phase):
        order, first, width = CHUNKS[c]
        t_ref, s_ref, u_ref, r1, r2, r3, ra, rb = per[8 * c : 8 * c + 8]
        result = []
        for k in (2, 1, 3):
            there, device = peer(order[phase], k)
            if phase == 0:
                source, target = t_ref.at[rows(there, 32)], r1.at[k - 1]
            elif phase == 1:
                source, target = s_ref.at[rows(there, 8)], r2.at[k - 1]
            else:
                source, target = u_ref.at[there], r3.at[k - 1]
            index = c * 12 + (phase * 3 + 3 if phase else 0) + k - 1
            result.append(remote(source, target, send_sems, recv_sems, index, device))
        return result

    def hops(c, step, begin=0, end=4):
        order, first, width = CHUNKS[c]
        t_ref, s_ref, u_ref, r1, r2, r3, ra, rb = per[8 * c : 8 * c + 8]
        cut = half(width)
        one, two = pl.ds(0, cut), pl.ds(cut, width - cut)
        far = peer(order[0], 2)[0]
        after, up = peer(order[0], 1)
        before, down = peer(order[0], 3)
        if step == 0:
            moves = [
                (t_ref.at[rows(far, 32), one], ra, up),
                (t_ref.at[rows(far, 32), two], rb, down),
                (t_ref.at[rows(after, 32), two], r1.at[0, :, two], up),
                (t_ref.at[rows(before, 32), one], r1.at[1, :, one], down),
            ]
        else:
            moves = [
                (t_ref.at[rows(after, 32), one], r1.at[0, :, one], up),
                (t_ref.at[rows(before, 32), two], r1.at[1, :, two], down),
            ]
        return [
            remote(source, target, send_sems, recv_sems, c * 12 + step * 4 + j, device)
            for j, (source, target, device) in enumerate(moves)
            if begin <= j < end
        ]

    def low_copies(n, phase):
        order = SETS[n][0]
        l_ref, k_ref, v_ref, s_ref, r1, r2 = low_per[6 * n : 6 * n + 6]
        result = []
        for k in (2, 1, 3):
            there, device = peer(order[phase], k)
            if phase == 0:
                source, target = v_ref.at[rows(there, 16)], r1.at[k - 1]
            else:
                source, target = s_ref.at[there], r2.at[k - 1]
            index = (n * 2 + phase) * 3 + k - 1
            result.append(remote(source, target, low_send, low_recv, index, device))
        return result

    def swap_copy(n):
        l_ref, k_ref = low_per[6 * n : 6 * n + 2]
        return remote(l_ref.at[rows(1 - core, 64)], k_ref, pair_send, pair_recv, n + 1, other)

    def ring_copies():
        result = []
        for k in (8, 7, 9, 6, 10, 5, 11, 4, 12, 3, 13, 2, 14, 1, 15):
            low, device = ring_peer(k)
            result.append(
                remote(ring_out.at[low], ring_in.at[k - 1], ring_send, ring_recv, k - 1, device)
            )
        return result

    def old_copy():
        return remote(old_ref.at[1 - core], old_in, pair_send, pair_recv, len(SETS) + 1, other)

    def pair_copy():
        return remote(pair_out, pair_in, pair_send, pair_recv, 0, other)

    def start(batch):
        for copy in batch:
            copy.start()

    def arrive(batch):
        for copy in batch:
            copy.wait_recv()

    def turn(c):
        order, first, width = CHUNKS[c]
        per[8 * c][...] = jnp.dot(
            turned[order], g_ref[:, first : first + width], preferred_element_type=jnp.float32
        )

    def low_first(n):
        order, first, count = SETS[n]
        place = band_permutation(order)
        parts = []
        for j in range(count):
            begin = (first + j) * GROUP
            both = jnp.dot(
                g_ref[:, begin : begin + GROUP], b_ref[...], preferred_element_type=jnp.float32
            )
            parts.append(both[:, :128] + both[:, 128:])
        high, low = split(jnp.concatenate(parts, axis=1))
        low_per[6 * n][...] = jnp.dot(place, high, preferred_element_type=jnp.float32) + jnp.dot(
            place, low, preferred_element_type=jnp.float32
        )
        swap_copy(n).start()

    def low_swapped(n):
        l_ref, k_ref, v_ref, s_ref, r1, r2 = low_per[6 * n : 6 * n + 6]
        arrive([swap_copy(n)])
        v_ref[...] = l_ref[rows(core, 64), :] + k_ref[...]
        start(low_copies(n, 0))

    def low_second(n):
        l_ref, k_ref, v_ref, s_ref, r1, r2 = low_per[6 * n : 6 * n + 6]
        arrive(low_copies(n, 0))
        total = (v_ref[rows(at[SETS[n][0][0]], 16), :] + r1[0]) + (r1[1] + r1[2])
        for q in range(4):
            s_ref[q] = total[4 * q : 4 * q + 4]
        start(low_copies(n, 1))

    def low_third(n):
        l_ref, k_ref, v_ref, s_ref, r1, r2 = low_per[6 * n : 6 * n + 6]
        order, first, count = SETS[n]
        arrive(low_copies(n, 1))
        total = (s_ref[at[order[1]]] + r2[0]) + (r2[1] + r2[2])
        for q in range(4):
            ring_out[q, :, first * 128 : (first + count) * 128] = total[q : q + 1]

    def relayed(c):
        order, first, width = CHUNKS[c]
        t_ref, s_ref, u_ref, r1, r2, r3, ra, rb = per[8 * c : 8 * c + 8]
        cut = half(width)
        arrive(hops(c, 0, 0, 2))
        after, before = rows(peer(order[0], 1)[0], 32), rows(peer(order[0], 3)[0], 32)
        t_ref[after, :cut] = t_ref[after, :cut] + ra[...]
        t_ref[before, cut:] = t_ref[before, cut:] + rb[...]
        start(hops(c, 1))

    def second(c):
        order, first, width = CHUNKS[c]
        t_ref, s_ref, u_ref, r1, r2, r3, ra, rb = per[8 * c : 8 * c + 8]
        own = rows(at[order[0]], 32)
        if order[0] == "z":
            arrive(copies(c, 0))
            s_ref[...] = (t_ref[own, :] + r1[0]) + (r1[1] + r1[2])
        else:
            arrive(hops(c, 0, 2) + hops(c, 1))
            s_ref[...] = t_ref[own, :] + (r1[0] + r1[1])
        start(copies(c, 1))

    def third(c):
        order, first, width = CHUNKS[c]
        t_ref, s_ref, u_ref, r1, r2, r3, ra, rb = per[8 * c : 8 * c + 8]
        arrive(copies(c, 1))
        own = pl.ds(pl.multiple_of(at[order[1]] * 8, 8), 8)
        total = (s_ref[own, :] + r2[0]) + (r2[1] + r2[2])
        for q in range(4):
            u_ref[q] = total[2 * q : 2 * q + 2]
        start(copies(c, 2))

    def last(c):
        order, first, width = CHUNKS[c]
        t_ref, s_ref, u_ref, r1, r2, r3, ra, rb = per[8 * c : 8 * c + 8]
        arrive(copies(c, 2))
        total = (u_ref[at[order[2]]] + r3[0]) + (r3[1] + r3[2])
        blended = DECAY * m_ref[:, first : first + width] + total
        begin = first
        while begin < first + width:
            g = begin // GROUP
            end = min(first + width, (g + 1) * GROUP)
            stack[2 * g : 2 * g + 2, begin - g * GROUP : end - g * GROUP] = blended[
                :, begin - first : end - first
            ]
            begin = end

    def low_fourth():
        arrive(ring_copies())
        terms = [ring_out[at["z"]]] + [ring_in[k] for k in range(RING - 1)]
        while len(terms) > 1:
            terms = [terms[j] + terms[j + 1] for j in range(0, len(terms), 2)]
        pair_out[...] = terms[0]
        pair_copy().start()

    def relay_signal(j):
        for k in (3, 13):
            pl.semaphore_signal(
                relay.at[j], inc=1, device_id=ring_peer(k)[1], device_id_type=MESH
            )

    def greet():
        for k, crosses, mine, theirs in crossing:

            @pl.when(jnp.logical_and(crosses, mine))
            def _():
                pl.semaphore_signal(relay.at[2], inc=1, device_id=across(k), device_id_type=MESH)

    def stage(number, when):
        @pl.when(when)
        def _():
            if number == 0:
                @pl.when(greetings > 0)
                def _():
                    pl.semaphore_wait(relay.at[2], greetings)

                relay_signal(0)
            elif number == 1:
                pl.semaphore_wait(relay.at[0], 2)
                relay_signal(1)
            else:
                pl.semaphore_wait(relay.at[1], 2)
                start(ring_copies())

    early, late = cube > 0, cube == 0
    loads[0].wait()
    turn(0)
    pl.semaphore_wait(barrier, entry)
    greet()
    start(hops(0, 0))
    loads[1].wait()
    turn(1)
    start(hops(1, 0))
    loads[2].wait()
    turn(2)
    start(copies(2, 0))
    b_load.wait()
    low_first(0)
    loads[3].wait()
    loads[4].wait()
    low_first(1)
    low_swapped(0)
    low_swapped(1)
    stage(0, early)
    for c in range(3, N_CHUNKS):
        turn(c)
    m_load.wait()
    high, low = b_ref[:, :128], b_ref[:, 128:]
    old = DECAY * m_ref[...]
    for g in range(GROUPS):
        stack[2 * g : 2 * g + 2, :] = old[:, g * GROUP : (g + 1) * GROUP]
    old_band = analyse(stack[...], high, low)
    for g in range(GROUPS):
        for i in range(2):
            old_ref[i, :, g * 128 : (g + 1) * 128] = old_band[2 * g + i : 2 * g + i + 1]
    start([old_copy()])
    relayed(0)
    relayed(1)
    start(hops(3, 0))
    start(hops(4, 0))
    for n in range(len(SETS)):
        low_second(n)
    stage(1, early)
    start(hops(5, 0))
    start(hops(6, 0))
    relayed(3)
    relayed(4)
    stage(0, late)
    for n in range(len(SETS)):
        low_third(n)
    arrive([old_copy()])
    ring_out[at["z"]] = ring_out[at["z"]] + (old_ref[core] + old_in[...])
    stage(2, early)
    second(0)
    second(1)
    second(2)
    stage(1, late)
    relayed(5)
    relayed(6)
    third(0)
    third(1)
    second(3)
    second(4)
    stage(2, late)
    third(2)
    second(5)
    second(6)
    last(0)
    last(1)
    third(3)
    third(4)
    last(2)
    third(5)
    third(6)
    low_fourth()
    last(3)
    last(4)
    last(5)
    last(6)
    blended = stack[...]
    fresh = blended - expand(analyse(blended, high, low), high, low)
    for g in range(GROUPS):
        fresh_ref[0, :, g * GROUP : (g + 1) * GROUP] = fresh[2 * g : 2 * g + 2]
    arrive([pair_copy()])
    for g in range(GROUPS):
        lanes = slice(g * 128, (g + 1) * 128)
        mine, theirs = pair_out[:, lanes], pair_in[:, lanes]
        band_stack[2 * g : 2 * g + 1, :] = jnp.where(core == 0, mine, theirs)
        band_stack[2 * g + 1 : 2 * g + 2, :] = jnp.where(core == 0, theirs, mine)
    update = expand(band_stack[...] * (1.0 / REPS), high, low)
    for g in range(GROUPS):
        update_ref[:, g * GROUP : (g + 1) * GROUP] = update[2 * g : 2 * g + 2]
    sent = []
    for c in range(N_CHUNKS):
        sent += copies(c, 0) if CHUNKS[c][0][0] == "z" else hops(c, 0) + hops(c, 1)
        sent += copies(c, 1) + copies(c, 2)
    sent += [copy for n in range(len(SETS)) for phase in range(2) for copy in low_copies(n, phase)]
    sent += ring_copies() + [pair_copy(), old_copy()] + [swap_copy(n) for n in range(len(SETS))]
    for copy in sent:
        copy.wait_send()


def shards(gradients, momentum):
    basis = jnp.asarray(halves())
    f32 = jnp.float32
    per = []
    for order, first, width in CHUNKS:
        per += [
            pltpu.VMEM((ROWS, width), f32),
            pltpu.VMEM((32, width), f32),
            pltpu.VMEM((4, 2, width), f32),
            pltpu.VMEM((3 if order[0] == "z" else 2, 32, width), f32),
            pltpu.VMEM((3, 8, width), f32),
            pltpu.VMEM((3, 2, width), f32),
            pltpu.VMEM((32, half(width)), f32),
            pltpu.VMEM((32, width - half(width)), f32),
        ]
    low_per = []
    for order, first, count in SETS:
        width = count * 128
        low_per += [
            pltpu.VMEM((ROWS, width), f32),
            pltpu.VMEM((64, width), f32),
            pltpu.VMEM((64, width), f32),
            pltpu.VMEM((4, 4, width), f32),
            pltpu.VMEM((3, 16, width), f32),
            pltpu.VMEM((3, 4, width), f32),
        ]
    return pl.pallas_call(
        kernel,
        out_shape=(
            jax.ShapeDtypeStruct((1, 2, D), f32),
            jax.ShapeDtypeStruct((2, D), f32),
        ),
        in_specs=[pl.BlockSpec(memory_space=pltpu.HBM)] * 3,
        out_specs=(pl.BlockSpec(memory_space=pltpu.VMEM),) * 2,
        scratch_shapes=[
            pltpu.VMEM((ROWS, D), jnp.bfloat16),
            pltpu.VMEM((2, D), f32),
            pltpu.VMEM((GROUP, 256), jnp.bfloat16),
            pltpu.VMEM((16, GROUP), f32),
            pltpu.VMEM((16, 128), f32),
            *per,
            *low_per,
            pltpu.VMEM((4, 1, BANDS), f32),
            pltpu.VMEM((RING - 1, 1, BANDS), f32),
            pltpu.VMEM((1, BANDS), f32),
            pltpu.VMEM((1, BANDS), f32),
            pltpu.VMEM((2, 1, BANDS), f32),
            pltpu.VMEM((1, BANDS), f32),
            pltpu.SemaphoreType.DMA((GROUPS + 2,)),
            pltpu.SemaphoreType.DMA((12 * N_CHUNKS,)),
            pltpu.SemaphoreType.DMA((12 * N_CHUNKS,)),
            pltpu.SemaphoreType.DMA((6 * len(SETS),)),
            pltpu.SemaphoreType.DMA((6 * len(SETS),)),
            pltpu.SemaphoreType.DMA((RING - 1,)),
            pltpu.SemaphoreType.DMA((RING - 1,)),
            pltpu.SemaphoreType.DMA((len(SETS) + 2,)),
            pltpu.SemaphoreType.DMA((len(SETS) + 2,)),
            pltpu.SemaphoreType.REGULAR((3,)),
        ],
        compiler_params=pltpu.CompilerParams(
            collective_id=0, has_side_effects=True, vmem_limit_bytes=55136 << 10
        ),
        name="momentum_step",
    )(gradients, momentum, basis)


def solution(mesh):
    return jax.shard_map(
        shards,
        mesh=mesh,
        in_specs=(P("rep", "fsdp", None, None), P("rep", "fsdp", None)),
        out_specs=(P("rep", "fsdp", None), P("fsdp", None)),
        check_vma=False,
    )
```

```python
import jax
import jax.numpy as jnp
import ml_dtypes
import numpy as np
from jax import lax
from jax.experimental import pallas as pl
from jax.experimental.pallas import tpu as pltpu
from jax.sharding import PartitionSpec as P

SPAN = 64
BAND = 8
D = 5120
ROWS = 128
GROUP = 1024
GROUPS = D // GROUP
DECAY = 0.9
MESH = pl.DeviceIdType.MESH

REPS = 8
RING = 16

CHUNKS = (
    ("xyz", 0, 896),
    ("yxz", 896, 896),
    ("zxy", 1792, 1280),
    ("xyz", 3072, 512),
    ("yxz", 3584, 512),
    ("xyz", 4096, 512),
    ("yxz", 4608, 512),
)
N_CHUNKS = len(CHUNKS)
SETS = (("xyz", 0, 2), ("yxz", 2, 3))
BANDS = D // SPAN * BAND


def halves():
    freq = np.arange(BAND)[:, None]
    place = np.arange(SPAN)[None, :]
    table = np.cos(np.pi * (2.0 * place + 1.0) * freq / (2.0 * SPAN)) * np.sqrt(2.0 / SPAN)
    table = table * np.where(freq == 0, np.sqrt(0.5), 1.0)
    full = np.zeros((GROUP, GROUP // SPAN * BAND), np.float32)
    for block in range(GROUP // SPAN):
        full[block * SPAN : (block + 1) * SPAN, block * BAND : (block + 1) * BAND] = table.T
    high = full.astype(ml_dtypes.bfloat16)
    low = (full - high.astype(np.float32)).astype(ml_dtypes.bfloat16)
    return np.concatenate([high, low], axis=1)


def half(width):
    return (width // 128 + 1) // 2 * 128


def selector(source):
    column = lax.broadcasted_iota(jnp.int32, (ROWS, ROWS), 1)
    return jnp.where(source == column, 1.0, 0.0).astype(jnp.bfloat16)


WEIGHT = {"y": 32, "z": 8, "x": 2}


def permutation(order):
    row = lax.broadcasted_iota(jnp.int32, (ROWS, ROWS), 0)
    return selector(
        ((row >> 5) & 3) * WEIGHT[order[0]]
        + ((row >> 3) & 3) * WEIGHT[order[1]]
        + ((row >> 1) & 3) * WEIGHT[order[2]]
        + (row & 1)
    )


def band_permutation(order):
    row = lax.broadcasted_iota(jnp.int32, (ROWS, ROWS), 0)
    return selector(
        ((row >> 4) & 3) * WEIGHT[order[0]]
        + ((row >> 2) & 3) * WEIGHT[order[1]]
        + (row & 3) * WEIGHT[order[2]]
        + (row >> 6)
    )


def split(value):
    high = value.astype(jnp.bfloat16)
    return high, (value - high.astype(jnp.float32)).astype(jnp.bfloat16)


def analyse(value, basis_high, basis_low):
    high, low = split(value)
    dims = (((1,), (0,)), ((), ()))
    f32 = jnp.float32
    return (
        lax.dot_general(high, basis_high, dims, preferred_element_type=f32)
        + lax.dot_general(high, basis_low, dims, preferred_element_type=f32)
        + lax.dot_general(low, basis_high, dims, preferred_element_type=f32)
    )


def expand(value, basis_high, basis_low):
    high, low = split(value)
    dims = (((1,), (1,)), ((), ()))
    f32 = jnp.float32
    return (
        lax.dot_general(high, basis_high, dims, preferred_element_type=f32)
        + lax.dot_general(high, basis_low, dims, preferred_element_type=f32)
        + lax.dot_general(low, basis_high, dims, preferred_element_type=f32)
    )


def kernel(g_hbm, m_hbm, b_hbm, fresh_ref, update_ref, *scratch):
    scratch = list(scratch)
    take = lambda n: [scratch.pop(0) for _ in range(n)]
    g_ref, m_ref, b_ref, stack, band_stack = take(5)
    per = take(8 * N_CHUNKS)
    low_per = take(6 * len(SETS))
    ring_out, ring_in, pair_out, pair_in, old_ref, old_in = take(6)
    load_sems, send_sems, recv_sems, low_send, low_recv = take(5)
    ring_send, ring_recv, pair_send, pair_recv, relay = take(5)

    rep = lax.axis_index("rep")
    fsdp = lax.axis_index("fsdp")
    core = rep % 2
    at = {"y": fsdp // 16, "z": (fsdp // 4) % 4, "x": fsdp % 4}
    stride = {"y": 16, "z": 4, "x": 1}
    height = (rep // 2) * 4 + at["z"]

    def peer(axis, k):
        there = lax.rem(at[axis] + k, 4)
        return there, {"rep": rep, "fsdp": fsdp + (there - at[axis]) * stride[axis]}

    def ring_peer(k):
        there = lax.rem(height + k, RING)
        low = there % 4
        return low, {"rep": (there // 4) * 2 + core, "fsdp": fsdp + (low - at["z"]) * 4}

    other = {"rep": rep + 1 - 2 * core, "fsdp": fsdp}

    cube, level = rep // 2, at["z"]
    waits_down, waits_up = cube >= 1, cube == 3
    crossing = [(k, level + k > 3, waits_up, cube < 3) for k in (1, 2, 3)]
    crossing += [(-k, level < k, waits_down, cube == 0) for k in (1, 2, 3)]

    def across(k):
        return ring_peer((k + RING) % RING)[1]

    barrier = pltpu.get_barrier_semaphore()
    for k, crosses, mine, theirs in crossing:

        @pl.when(jnp.logical_and(crosses, theirs))
        def _():
            pl.semaphore_signal(barrier, inc=1, device_id=across(k), device_id_type=MESH)

    for k in (2, 1, 3):
        for axis in "zxy":
            pl.semaphore_signal(barrier, inc=1, device_id=peer(axis, k)[1], device_id_type=MESH)
    pl.semaphore_signal(barrier, inc=1, device_id=other, device_id_type=MESH)
    entry = 10 + jnp.where(waits_down, 3 - level, 0) + jnp.where(waits_up, level, 0)
    greetings = jnp.where(waits_down, 0, 3 - level) + jnp.where(waits_up, 0, level)

    loads = []
    for g in range(GROUPS):
        columns = pl.ds(g * GROUP, GROUP)
        loads.append(
            pltpu.make_async_copy(g_hbm.at[0, 0, :, columns], g_ref.at[:, columns], load_sems.at[g])
        )
    b_load = pltpu.make_async_copy(b_hbm, b_ref, load_sems.at[GROUPS + 1])
    m_load = pltpu.make_async_copy(m_hbm.at[0], m_ref, load_sems.at[GROUPS])
    b_load.start()
    for load in loads:
        load.start()
    m_load.start()

    turned = {order: permutation(order) for order in ("xyz", "yxz", "zxy")}
    stack[...] = jnp.zeros_like(stack)
    band_stack[...] = jnp.zeros_like(band_stack)

    def remote(source, target, sends, recvs, index, device):
        return pltpu.make_async_remote_copy(
            src_ref=source,
            dst_ref=target,
            send_sem=sends.at[index],
            recv_sem=recvs.at[index],
            device_id=device,
            device_id_type=MESH,
        )

    def rows(place, count):
        return pl.ds(pl.multiple_of(place * count, count), count)

    def copies(c, phase):
        order, first, width = CHUNKS[c]
        t_ref, s_ref, u_ref, r1, r2, r3, ra, rb = per[8 * c : 8 * c + 8]
        result = []
        for k in (2, 1, 3):
            there, device = peer(order[phase], k)
            if phase == 0:
                source, target = t_ref.at[rows(there, 32)], r1.at[k - 1]
            elif phase == 1:
                source, target = s_ref.at[rows(there, 8)], r2.at[k - 1]
            else:
                source, target = u_ref.at[there], r3.at[k - 1]
            index = c * 12 + (phase * 3 + 3 if phase else 0) + k - 1
            result.append(remote(source, target, send_sems, recv_sems, index, device))
        return result

    def hops(c, step, begin=0, end=4):
        order, first, width = CHUNKS[c]
        t_ref, s_ref, u_ref, r1, r2, r3, ra, rb = per[8 * c : 8 * c + 8]
        cut = half(width)
        one, two = pl.ds(0, cut), pl.ds(cut, width - cut)
        far = peer(order[0], 2)[0]
        after, up = peer(order[0], 1)
        before, down = peer(order[0], 3)
        if step == 0:
            moves = [
                (t_ref.at[rows(far, 32), one], ra, up),
                (t_ref.at[rows(far, 32), two], rb, down),
                (t_ref.at[rows(after, 32), two], r1.at[0, :, two], up),
                (t_ref.at[rows(before, 32), one], r1.at[1, :, one], down),
            ]
        else:
            moves = [
                (t_ref.at[rows(after, 32), one], r1.at[0, :, one], up),
                (t_ref.at[rows(before, 32), two], r1.at[1, :, two], down),
            ]
        return [
            remote(source, target, send_sems, recv_sems, c * 12 + step * 4 + j, device)
            for j, (source, target, device) in enumerate(moves)
            if begin <= j < end
        ]

    def low_copies(n, phase):
        order = SETS[n][0]
        l_ref, k_ref, v_ref, s_ref, r1, r2 = low_per[6 * n : 6 * n + 6]
        result = []
        for k in (2, 1, 3):
            there, device = peer(order[phase], k)
            if phase == 0:
                source, target = v_ref.at[rows(there, 16)], r1.at[k - 1]
            else:
                source, target = s_ref.at[there], r2.at[k - 1]
            index = (n * 2 + phase) * 3 + k - 1
            result.append(remote(source, target, low_send, low_recv, index, device))
        return result

    def swap_copy(n):
        l_ref, k_ref = low_per[6 * n : 6 * n + 2]
        return remote(l_ref.at[rows(1 - core, 64)], k_ref, pair_send, pair_recv, n + 1, other)

    def ring_copies():
        result = []
        for k in (8, 7, 9, 6, 10, 5, 11, 4, 12, 3, 13, 2, 14, 1, 15):
            low, device = ring_peer(k)
            result.append(
                remote(ring_out.at[low], ring_in.at[k - 1], ring_send, ring_recv, k - 1, device)
            )
        return result

    def old_copy():
        return remote(old_ref.at[1 - core], old_in, pair_send, pair_recv, len(SETS) + 1, other)

    def pair_copy():
        return remote(pair_out, pair_in, pair_send, pair_recv, 0, other)

    def start(batch):
        for copy in batch:
            copy.start()

    def arrive(batch):
        for copy in batch:
            copy.wait_recv()

    def turn(c):
        order, first, width = CHUNKS[c]
        per[8 * c][...] = jnp.dot(
            turned[order], g_ref[:, first : first + width], preferred_element_type=jnp.float32
        )

    def low_first(n):
        order, first, count = SETS[n]
        place = band_permutation(order)
        parts = []
        for j in range(count):
            begin = (first + j) * GROUP
            both = jnp.dot(
                g_ref[:, begin : begin + GROUP], b_ref[...], preferred_element_type=jnp.float32
            )
            parts.append(both[:, :128] + both[:, 128:])
        high, low = split(jnp.concatenate(parts, axis=1))
        low_per[6 * n][...] = jnp.dot(place, high, preferred_element_type=jnp.float32) + jnp.dot(
            place, low, preferred_element_type=jnp.float32
        )
        swap_copy(n).start()

    def low_swapped(n):
        l_ref, k_ref, v_ref, s_ref, r1, r2 = low_per[6 * n : 6 * n + 6]
        arrive([swap_copy(n)])
        v_ref[...] = l_ref[rows(core, 64), :] + k_ref[...]
        start(low_copies(n, 0))

    def low_second(n):
        l_ref, k_ref, v_ref, s_ref, r1, r2 = low_per[6 * n : 6 * n + 6]
        arrive(low_copies(n, 0))
        total = (v_ref[rows(at[SETS[n][0][0]], 16), :] + r1[0]) + (r1[1] + r1[2])
        for q in range(4):
            s_ref[q] = total[4 * q : 4 * q + 4]
        start(low_copies(n, 1))

    def low_third(n):
        l_ref, k_ref, v_ref, s_ref, r1, r2 = low_per[6 * n : 6 * n + 6]
        order, first, count = SETS[n]
        arrive(low_copies(n, 1))
        total = (s_ref[at[order[1]]] + r2[0]) + (r2[1] + r2[2])
        for q in range(4):
            ring_out[q, :, first * 128 : (first + count) * 128] = total[q : q + 1]

    def relayed(c):
        order, first, width = CHUNKS[c]
        t_ref, s_ref, u_ref, r1, r2, r3, ra, rb = per[8 * c : 8 * c + 8]
        cut = half(width)
        arrive(hops(c, 0, 0, 2))
        after, before = rows(peer(order[0], 1)[0], 32), rows(peer(order[0], 3)[0], 32)
        t_ref[after, :cut] = t_ref[after, :cut] + ra[...]
        t_ref[before, cut:] = t_ref[before, cut:] + rb[...]
        start(hops(c, 1))

    def second(c):
        order, first, width = CHUNKS[c]
        t_ref, s_ref, u_ref, r1, r2, r3, ra, rb = per[8 * c : 8 * c + 8]
        own = rows(at[order[0]], 32)
        if order[0] == "z":
            arrive(copies(c, 0))
            s_ref[...] = (t_ref[own, :] + r1[0]) + (r1[1] + r1[2])
        else:
            arrive(hops(c, 0, 2) + hops(c, 1))
            s_ref[...] = t_ref[own, :] + (r1[0] + r1[1])
        start(copies(c, 1))

    def third(c):
        order, first, width = CHUNKS[c]
        t_ref, s_ref, u_ref, r1, r2, r3, ra, rb = per[8 * c : 8 * c + 8]
        arrive(copies(c, 1))
        own = pl.ds(pl.multiple_of(at[order[1]] * 8, 8), 8)
        total = (s_ref[own, :] + r2[0]) + (r2[1] + r2[2])
        for q in range(4):
            u_ref[q] = total[2 * q : 2 * q + 2]
        start(copies(c, 2))

    def last(c):
        order, first, width = CHUNKS[c]
        t_ref, s_ref, u_ref, r1, r2, r3, ra, rb = per[8 * c : 8 * c + 8]
        arrive(copies(c, 2))
        total = (u_ref[at[order[2]]] + r3[0]) + (r3[1] + r3[2])
        blended = DECAY * m_ref[:, first : first + width] + total
        begin = first
        while begin < first + width:
            g = begin // GROUP
            end = min(first + width, (g + 1) * GROUP)
            stack[2 * g : 2 * g + 2, begin - g * GROUP : end - g * GROUP] = blended[
                :, begin - first : end - first
            ]
            begin = end

    def low_fourth():
        arrive(ring_copies())
        terms = [ring_out[at["z"]]] + [ring_in[k] for k in range(RING - 1)]
        while len(terms) > 1:
            terms = [terms[j] + terms[j + 1] for j in range(0, len(terms), 2)]
        pair_out[...] = terms[0]
        pair_copy().start()

    def relay_signal(j):
        for k in (3, 13):
            pl.semaphore_signal(
                relay.at[j], inc=1, device_id=ring_peer(k)[1], device_id_type=MESH
            )

    def greet():
        for k, crosses, mine, theirs in crossing:

            @pl.when(jnp.logical_and(crosses, mine))
            def _():
                pl.semaphore_signal(relay.at[2], inc=1, device_id=across(k), device_id_type=MESH)

    def stage(number, when):
        @pl.when(when)
        def _():
            if number == 0:
                @pl.when(greetings > 0)
                def _():
                    pl.semaphore_wait(relay.at[2], greetings)

                relay_signal(0)
            elif number == 1:
                pl.semaphore_wait(relay.at[0], 2)
                relay_signal(1)
            else:
                pl.semaphore_wait(relay.at[1], 2)
                start(ring_copies())

    early, late = cube > 0, cube == 0
    loads[0].wait()
    turn(0)
    pl.semaphore_wait(barrier, entry)
    greet()
    start(hops(0, 0))
    loads[1].wait()
    turn(1)
    start(hops(1, 0))
    loads[2].wait()
    turn(2)
    start(copies(2, 0))
    b_load.wait()
    low_first(0)
    loads[3].wait()
    loads[4].wait()
    low_first(1)
    low_swapped(0)
    low_swapped(1)
    stage(0, early)
    for c in range(3, N_CHUNKS):
        turn(c)
    m_load.wait()
    high, low = b_ref[:, :128], b_ref[:, 128:]
    old = DECAY * m_ref[...]
    for g in range(GROUPS):
        stack[2 * g : 2 * g + 2, :] = old[:, g * GROUP : (g + 1) * GROUP]
    old_band = analyse(stack[...], high, low)
    for g in range(GROUPS):
        for i in range(2):
            old_ref[i, :, g * 128 : (g + 1) * 128] = old_band[2 * g + i : 2 * g + i + 1]
    start([old_copy()])
    relayed(0)
    relayed(1)
    start(hops(3, 0))
    start(hops(4, 0))
    for n in range(len(SETS)):
        low_second(n)
    stage(1, early)
    start(hops(5, 0))
    start(hops(6, 0))
    relayed(3)
    relayed(4)
    stage(0, late)
    for n in range(len(SETS)):
        low_third(n)
    arrive([old_copy()])
    ring_out[at["z"]] = ring_out[at["z"]] + (old_ref[core] + old_in[...])
    stage(2, early)
    second(0)
    second(1)
    second(2)
    stage(1, late)
    relayed(5)
    relayed(6)
    third(0)
    third(1)
    second(3)
    second(4)
    stage(2, late)
    third(2)
    second(5)
    second(6)
    last(0)
    last(1)
    third(3)
    third(4)
    last(2)
    third(5)
    third(6)
    low_fourth()
    last(3)
    last(4)
    last(5)
    last(6)
    blended = stack[...]
    fresh = blended - expand(analyse(blended, high, low), high, low)
    for g in range(GROUPS):
        fresh_ref[0, :, g * GROUP : (g + 1) * GROUP] = fresh[2 * g : 2 * g + 2]
    arrive([pair_copy()])
    for g in range(GROUPS):
        lanes = slice(g * 128, (g + 1) * 128)
        mine, theirs = pair_out[:, lanes], pair_in[:, lanes]
        band_stack[2 * g : 2 * g + 1, :] = jnp.where(core == 0, mine, theirs)
        band_stack[2 * g + 1 : 2 * g + 2, :] = jnp.where(core == 0, theirs, mine)
    update = expand(band_stack[...] * (1.0 / REPS), high, low)
    for g in range(GROUPS):
        update_ref[:, g * GROUP : (g + 1) * GROUP] = update[2 * g : 2 * g + 2]
    sent = []
    for c in range(N_CHUNKS):
        sent += copies(c, 0) if CHUNKS[c][0][0] == "z" else hops(c, 0) + hops(c, 1)
        sent += copies(c, 1) + copies(c, 2)
    sent += [copy for n in range(len(SETS)) for phase in range(2) for copy in low_copies(n, phase)]
    sent += ring_copies() + [pair_copy(), old_copy()] + [swap_copy(n) for n in range(len(SETS))]
    for copy in sent:
        copy.wait_send()


def shards(gradients, momentum):
    basis = jnp.asarray(halves())
    f32 = jnp.float32
    per = []
    for order, first, width in CHUNKS:
        per += [
            pltpu.VMEM((ROWS, width), f32),
            pltpu.VMEM((32, width), f32),
            pltpu.VMEM((4, 2, width), f32),
            pltpu.VMEM((3 if order[0] == "z" else 2, 32, width), f32),
            pltpu.VMEM((3, 8, width), f32),
            pltpu.VMEM((3, 2, width), f32),
            pltpu.VMEM((32, half(width)), f32),
            pltpu.VMEM((32, width - half(width)), f32),
        ]
    low_per = []
    for order, first, count in SETS:
        width = count * 128
        low_per += [
            pltpu.VMEM((ROWS, width), f32),
            pltpu.VMEM((64, width), f32),
            pltpu.VMEM((64, width), f32),
            pltpu.VMEM((4, 4, width), f32),
            pltpu.VMEM((3, 16, width), f32),
            pltpu.VMEM((3, 4, width), f32),
        ]
    return pl.pallas_call(
        kernel,
        out_shape=(
            jax.ShapeDtypeStruct((1, 2, D), f32),
            jax.ShapeDtypeStruct((2, D), f32),
        ),
        in_specs=[pl.BlockSpec(memory_space=pltpu.HBM)] * 3,
        out_specs=(pl.BlockSpec(memory_space=pltpu.VMEM),) * 2,
        scratch_shapes=[
            pltpu.VMEM((ROWS, D), jnp.bfloat16),
            pltpu.VMEM((2, D), f32),
            pltpu.VMEM((GROUP, 256), jnp.bfloat16),
            pltpu.VMEM((16, GROUP), f32),
            pltpu.VMEM((16, 128), f32),
            *per,
            *low_per,
            pltpu.VMEM((4, 1, BANDS), f32),
            pltpu.VMEM((RING - 1, 1, BANDS), f32),
            pltpu.VMEM((1, BANDS), f32),
            pltpu.VMEM((1, BANDS), f32),
            pltpu.VMEM((2, 1, BANDS), f32),
            pltpu.VMEM((1, BANDS), f32),
            pltpu.SemaphoreType.DMA((GROUPS + 2,)),
            pltpu.SemaphoreType.DMA((12 * N_CHUNKS,)),
            pltpu.SemaphoreType.DMA((12 * N_CHUNKS,)),
            pltpu.SemaphoreType.DMA((6 * len(SETS),)),
            pltpu.SemaphoreType.DMA((6 * len(SETS),)),
            pltpu.SemaphoreType.DMA((RING - 1,)),
            pltpu.SemaphoreType.DMA((RING - 1,)),
            pltpu.SemaphoreType.DMA((len(SETS) + 2,)),
            pltpu.SemaphoreType.DMA((len(SETS) + 2,)),
            pltpu.SemaphoreType.REGULAR((3,)),
        ],
        compiler_params=pltpu.CompilerParams(
            collective_id=0, has_side_effects=True, vmem_limit_bytes=55136 << 10
        ),
        name="momentum_step",
    )(gradients, momentum, basis)


def solution(mesh):
    return jax.shard_map(
        shards,
        mesh=mesh,
        in_specs=(P("rep", "fsdp", None, None), P("rep", "fsdp", None)),
        out_specs=(P("rep", "fsdp", None), P("fsdp", None)),
        check_vma=False,
    )
```
